128 devices in a mesh: side: 2 (over y_hi), row: 8 (over x, y_lo), col: 8 (over z, core).
Axes of the slice: x: 4, y: 4 (y_hi: 2, y_lo: 2; y = y_hi * 2 + y_lo), z: 4, core: 2. Of those that a mesh axis runs over, the one named last changes fastest.
Arguments:
- query_rows: bfloat16 [512, 16384], P(('side', 'row'), 'col'), may hold values from -60 to 60
- key_cache: bfloat16 [512, 256, 1024], P(('side', 'row'), None, 'col'), may hold values from -15 to 15
- value_cache: bfloat16 [512, 256, 1024], P(('side', 'row'), None, 'col'), may hold values from -6 to 6
- cache_lengths: int32 [512], P(('side', 'row')), may hold values from 2 to 256, as said below
- residual_in: bfloat16 [512, 16384], P(('side', 'row'), 'col'), may hold values from -90 to 90
- norm_gain: float32 [16384], replicated, may hold values from 0.5 to 1.5
- outlier_index: int32 [64], replicated, may hold values from 0 to 16383, as said below
- gate_weight: bfloat16 [16384, 26624], P('row', ('side', 'col')), may hold values from -0.046875 to 0.046875
- up_weight: bfloat16 [16384, 26624], P('row', ('side', 'col')), may hold values from -0.046875 to 0.046875
- down_weight: bfloat16 [26624, 16384], P(('side', 'col'), 'row'), may hold values from -0.0390625 to 0.0390625
Outputs:
- layer_out: bfloat16 [512, 16384], P(('side', 'row'), 'col')
The draws below stay inside these ranges and needn't reach their ends.
Inputs may be any that keep to these rules, and one draw needn't show every extreme that they name: Row i attends to cache entries 0 to cache_lengths[i] - 1; every row whose index is a multiple of 8 is full. `outlier_index`: 64 distinct channels.
All inputs are finite; a program needn't handle non-finite values.
Results may differ from the reference program's by a relative error of at most 0.012.
Values may be sent and summed in bfloat16 or wider, within the bound.
A program may use at most 128 MiB of HBM per device.

```python
import jax
import jax.numpy as jnp
from jax import lax

HEADS = 128
KV_HEADS = 8
HD = 128
D = 16384
FF = 26624
NOUT = 64
L = 256
ROWS = 512


def shared_outliers(key):
    return jax.random.permutation(jax.random.fold_in(key, 71), D)[:NOUT].astype(jnp.int32)


def shared_keys(key):
    base_keys = jnp.clip(jax.random.normal(jax.random.fold_in(key, 53), (ROWS, L, KV_HEADS * HD), jnp.float32), -6.0, 6.0)
    aligned = (jnp.arange(ROWS) % 8 == 0)[:, None]
    lead_keys = base_keys[:, 0, :]
    next_keys = base_keys[:, 1, :]
    new_lead = jnp.where(aligned, lead_keys, lead_keys)
    new_next = jnp.where(aligned, next_keys, next_keys)
    return base_keys.at[:, 0, :].set(new_lead).at[:, 1, :].set(new_next)


def draw_key_cache(key, part):
    return shared_keys(key).astype(jnp.bfloat16)


def draw_query_rows(key, part):
    strength = 0.0
    key = jax.random.fold_in(key, 3)
    drawn = jnp.clip(jax.random.normal(key, (ROWS, HEADS * HD), jnp.float32), -6.0, 6.0)
    aligned = strength * (jnp.arange(ROWS) % 8 == 0).astype(jnp.float32)[:, None]
    return (drawn * (1.0 - aligned)).astype(jnp.bfloat16)


def draw_cache_lengths(key, part):
    key = jax.random.fold_in(key, 4)
    random_len = jax.random.randint(key, (ROWS,), 2, L + 1).astype(jnp.int32)
    return jnp.where(jnp.arange(ROWS) % 8 == 0, L, random_len).astype(jnp.int32)


def draw_outlier_index(key, part):
    return shared_outliers(key)


def draw_residual_in(key, part):
    picked = shared_outliers(key)
    key = jax.random.fold_in(key, 2)
    key_base, key_size, key_sign = jax.random.split(key, 3)
    base_values = jnp.clip(jax.random.normal(key_base, (ROWS, D), jnp.float32), -6.0, 6.0)
    signs = jnp.where(jax.random.normal(key_sign, (1, NOUT), jnp.float32) > 0.0, 1.0, -1.0)
    spikes = signs * jax.random.uniform(key_size, (ROWS, NOUT), jnp.float32, 10.0, 30.0)
    return base_values.at[:, picked].set(spikes).astype(jnp.bfloat16)


def level_of(stream_key, dims, cuts, low, top_value):
    def one(dim, blocks):
        draws = jax.random.uniform(jax.random.fold_in(jax.random.fold_in(stream_key, 6), dim), (blocks,), jnp.float32, low / len(cuts), top_value / len(cuts))
        return jnp.repeat(jnp.exp(draws), dims[dim] // blocks).reshape((-1,) + (1,) * (len(dims) - dim - 1))

    gain = one(*cuts[0])
    for cut in cuts[1:]:
        gain = gain * one(*cut)
    return gain


def bell_draw(stream_key, extent, deviation, most, cuts=(), held_as=jnp.bfloat16):
    loudness = level_of(stream_key, extent, cuts, -0.22, 0.18) if cuts else 1.0
    values = jax.random.normal(stream_key, extent, jnp.float32) * deviation * loudness
    return jnp.minimum(jnp.maximum(values, -most), most).astype(held_as)


def setup_inputs(seed: int = 0) -> dict:
    key_list = jax.random.split(jax.random.key(seed), 11)
    query_rows = draw_query_rows(jax.random.fold_in(key_list[10], 71), 0)
    key_cache = draw_key_cache(jax.random.fold_in(key_list[10], 71), 0)
    value_cache = bell_draw(key_list[2], (ROWS, L, KV_HEADS * HD), 1.0, 6.0, ((0, 16), (2, 8)))
    cache_lengths = draw_cache_lengths(jax.random.fold_in(key_list[10], 71), 0)
    residual_in = draw_residual_in(jax.random.fold_in(key_list[10], 71), 0)
    norm_gain = jnp.clip(1.0 + 0.1 * jax.random.normal(key_list[5], (D,), jnp.float32), 0.5, 1.5)
    outlier_index = draw_outlier_index(jax.random.fold_in(key_list[10], 71), 0)
    gate_weight = bell_draw(key_list[7], (D, FF), D ** -0.5, 0.046875, ((0, 8), (1, 16)))
    up_weight = bell_draw(key_list[8], (D, FF), D ** -0.5, 0.046875, ((0, 8), (1, 16)))
    down_weight = bell_draw(key_list[9], (FF, D), FF ** -0.5, 0.0390625, ((0, 16), (1, 8)))
    return dict(query_rows=query_rows, key_cache=key_cache, value_cache=value_cache, cache_lengths=cache_lengths, residual_in=residual_in, norm_gain=norm_gain, outlier_index=outlier_index, gate_weight=gate_weight, up_weight=up_weight, down_weight=down_weight)


def reference(query_rows, key_cache, value_cache, cache_lengths, residual_in, norm_gain, outlier_index, gate_weight, up_weight, down_weight):
    group_size = HEADS // KV_HEADS
    query_f = query_rows.astype(jnp.float32).reshape(ROWS, KV_HEADS, group_size, HD)
    key_f = key_cache.astype(jnp.float32).reshape(ROWS, L, KV_HEADS, HD)
    value_f = value_cache.astype(jnp.float32).reshape(ROWS, L, KV_HEADS, HD)
    scores = jnp.einsum('igqd,itgd->igqt', query_f, key_f) * HD ** (-0.5)
    valid_mask = jnp.arange(L, dtype=jnp.int32)[None, :] < cache_lengths[:, None]
    scores = jnp.where(valid_mask[:, None, None, :], scores, -1e+30)
    top_score = lax.optimization_barrier(jnp.max(scores, axis=-1, keepdims=True))
    expon = jnp.exp(scores - top_score)
    attn_probs = (expon / lax.optimization_barrier(jnp.sum(expon, axis=-1, keepdims=True))).astype(jnp.bfloat16)
    attention = jnp.einsum('igqt,itgd->igqd', attn_probs.astype(jnp.float32), value_f).reshape(ROWS, D)
    residual = (residual_in.astype(jnp.float32) + attention).astype(jnp.bfloat16)
    resid_f = residual.astype(jnp.float32)
    root_mean = jnp.sqrt(lax.optimization_barrier(jnp.mean(resid_f * resid_f, axis=1, keepdims=True)) + 1e-05)
    normed = resid_f / root_mean * norm_gain[None, :]
    is_outlier = jnp.any(jnp.arange(D, dtype=jnp.int32)[:, None] == outlier_index[None, :], axis=1)
    inliers = jnp.where(is_outlier[None, :], 0.0, jnp.clip(normed, -3.0, 3.0)).astype(jnp.bfloat16)
    outliers = jnp.take(normed, outlier_index, axis=1)
    gate_rows = jnp.take(gate_weight, outlier_index, axis=0).astype(jnp.float32)
    up_rows = jnp.take(up_weight, outlier_index, axis=0).astype(jnp.float32)
    gate = jnp.dot(inliers, gate_weight, preferred_element_type=jnp.float32) + jnp.dot(outliers, gate_rows, precision=lax.Precision.HIGHEST)
    up = jnp.dot(inliers, up_weight, preferred_element_type=jnp.float32) + jnp.dot(outliers, up_rows, precision=lax.Precision.HIGHEST)
    hidden = (jax.nn.silu(gate) * up).astype(jnp.bfloat16)
    ffn = jnp.dot(hidden, down_weight, preferred_element_type=jnp.float32)
    return (residual.astype(jnp.float32) + ffn).astype(jnp.bfloat16)
```

```python
import functools

import jax
import jax.numpy as jnp
from jax import lax
from jax.experimental import pallas as pl
from jax.experimental.pallas import tpu as pltpu
from jax.sharding import PartitionSpec as P

HD = 128
MESH = pl.DeviceIdType.MESH
STRIPE = 16
TILE = 256
NX = 4
NZ = 4
ORDER = (0, 1, 3, 2)


def ffn_kernel(
    cfg,
    res_ref,
    sq_ref,
    gain_ref,
    mask_ref,
    gate_hbm,
    up_hbm,
    down_hbm,
    out_ref,
    w_in,
    w_out,
    turned,
    sq_buf,
    xbuf,
    gbuf,
    rx1,
    sx,
    rx2,
    ry1,
    sy,
    ry2,
    hbuf,
    obuf,
    rcore,
    osum,
    rz,
    fpeer,
    rside,
    fin,
    rfin,
    w_sem,
    send_sem,
    recv_sem,
    loc_sem,
):
    rows, width, hid = cfg["rows"], cfg["width"], cfg["hid"]
    split_in, split_hid = cfg["split_in"], cfg["split_hid"]
    both = 2 * hid
    s, r, c = lax.axis_index("side"), lax.axis_index("row"), lax.axis_index("col")
    x, p = r // 2, lax.rem(r, 2)
    z, k = c // 2, lax.rem(c, 2)
    diagonal = r == c

    def x_peer(d):
        return (s, lax.rem(x + d, NX) * 2 + p, c)

    def z_peer(d):
        return (s, r, lax.rem(z + d, NZ) * 2 + k)

    y_peer = (s, x * 2 + 1 - p, c)
    side_peer = (1 - s, r, c)
    core_peer = (s, r, z * 2 + 1 - k)
    turn_peer = (s, c, r)

    ids = {}

    def copy(name, src, dst, device):
        i = ids.setdefault(name, len(ids))
        return pltpu.make_async_remote_copy(
            src_ref=src,
            dst_ref=dst,
            send_sem=send_sem.at[i],
            recv_sem=recv_sem.at[i],
            device_id=device,
            device_id_type=MESH,
        )

    sent = []

    def send(name, src, dst, device):
        cp = copy(name, src, dst, device)
        cp.start()
        sent.append(cp)

    def arrive(name, dst):
        copy(name, dst, dst, core_peer).wait_recv()

    w_copies = [
        pltpu.make_async_copy(gate_hbm, w_in.at[:, pl.ds(0, hid)], w_sem.at[0]),
        pltpu.make_async_copy(up_hbm, w_in.at[:, pl.ds(hid, hid)], w_sem.at[1]),
        pltpu.make_async_copy(down_hbm, w_out, w_sem.at[2]),
    ]
    for cp in w_copies:
        cp.start()

    barrier = pltpu.get_barrier_semaphore()
    greet = [x_peer(d) for d in range(1, NX)] + [z_peer(d) for d in range(1, NZ)]
    greet += [y_peer, side_peer, core_peer]
    for device in greet:
        pl.semaphore_signal(barrier, inc=1, device_id=device, device_id_type=MESH)
    for j in range(8):

        @pl.when(jnp.logical_not(jnp.logical_and(diagonal, j == r)))
        def _():
            pl.semaphore_signal(barrier, inc=1, device_id=(s, c, j), device_id_type=MESH)

    pl.semaphore_wait(barrier, len(greet) + 8 - diagonal.astype(jnp.int32))

    turn = copy("turn", res_ref, turned, turn_peer)
    turn_here = pltpu.make_async_copy(res_ref, turned, loc_sem.at[0])
    sq_here = pltpu.make_async_copy(sq_ref, sq_buf.at[c], loc_sem.at[1])
    sq_out = []
    for j in range(8):
        cp = pltpu.make_async_remote_copy(
            src_ref=sq_ref,
            dst_ref=sq_buf.at[c],
            send_sem=send_sem.at[cfg["sq0"] + j],
            recv_sem=recv_sem.at[cfg["sq0"] + c],
            device_id=(s, j, r),
            device_id_type=MESH,
        )
        sq_out.append(cp)

        @pl.when(jnp.logical_not(jnp.logical_and(diagonal, j == r)))
        def _():
            cp.start()

    @pl.when(diagonal)
    def _():
        turn_here.start()
        sq_here.start()
        turn_here.wait()
        sq_here.wait()

    @pl.when(jnp.logical_not(diagonal))
    def _():
        turn.start()

    for j in range(8):

        @pl.when(jnp.logical_not(jnp.logical_and(diagonal, j == c)))
        def _():
            pltpu.make_async_remote_copy(
                src_ref=sq_ref,
                dst_ref=sq_buf.at[j],
                send_sem=send_sem.at[cfg["sq0"] + j],
                recv_sem=recv_sem.at[cfg["sq0"] + j],
                device_id=core_peer,
                device_id_type=MESH,
            ).wait_recv()

    sq_row = jnp.sum(sq_buf[...], axis=0)[0:1, :]
    eye = lax.broadcasted_iota(jnp.int32, (rows, 128), 0) == lax.broadcasted_iota(
        jnp.int32, (rows, 128), 1
    )
    sq_col = jnp.sum(
        jnp.where(eye, jnp.broadcast_to(sq_row, (rows, 128)), 0.0), axis=1, keepdims=True
    )
    inv = 1.0 / jnp.sqrt(sq_col / cfg["model"] + 1e-5)

    @pl.when(jnp.logical_not(diagonal))
    def _():
        turn.wait_recv()

    normed = turned[...].astype(jnp.float32) * inv * gain_ref[...]
    kept = jnp.where(mask_ref[...] > 0.5, normed, jnp.clip(normed, -3.0, 3.0))
    xbuf[0, k, s] = kept.astype(jnp.bfloat16)

    send("g_side", xbuf.at[0, k, s], xbuf.at[0, k, s], side_peer)
    for d in (1, 3, 2):
        send(f"g_z{d}a", xbuf.at[0, k, s], xbuf.at[NZ - d, k, s], z_peer(d))
    send("g_c0a", xbuf.at[0, k, s], xbuf.at[0, k, s], core_peer)
    arrive("g_side", xbuf.at[0, k, 1 - s])
    for d in (1, 3, 2):
        send(f"g_z{d}b", xbuf.at[0, k, 1 - s], xbuf.at[NZ - d, k, 1 - s], z_peer(d))
    send("g_c0b", xbuf.at[0, k, 1 - s], xbuf.at[0, k, 1 - s], core_peer)

    def forward(e):
        d = NZ - e
        arrive(f"g_z{d}a", xbuf.at[e, k, s])
        send(f"g_c{e}a", xbuf.at[e, k, s], xbuf.at[e, k, s], core_peer)
        arrive(f"g_z{d}b", xbuf.at[e, k, 1 - s])
        send(f"g_c{e}b", xbuf.at[e, k, 1 - s], xbuf.at[e, k, 1 - s], core_peer)

    def ready(e):
        arrive(f"g_c{e}a", xbuf.at[e, 1 - k, s])
        arrive(f"g_c{e}b", xbuf.at[e, 1 - k, 1 - s])

    def into_gate_up(e, lo, hi):
        def tile(t, carry):
            cols = pl.ds(pl.multiple_of(t * TILE, TILE), TILE)
            part = jnp.dot(
                xbuf[e].reshape(4 * rows, width),
                w_in[:, cols],
                preferred_element_type=jnp.float32,
            )
            gbuf[e, :, :, :, cols] = part.astype(jnp.bfloat16).reshape(2, NX, STRIPE, TILE)
            return carry

        lax.fori_loop(lo, hi, tile, 0)

    left, right = pl.ds(0, split_in), pl.ds(split_in, both - split_in)

    def reduce_1(e):
        for d in (2, 1, 3):
            send(
                f"rx1_{e}_{d}",
                gbuf.at[e, :, lax.rem(x + d, NX), :, left],
                rx1.at[e, d - 1],
                x_peer(d),
            )
        send(f"ry1_{e}", gbuf.at[e, 1 - p, :, :, right], ry1.at[e], y_peer)

    def f32(value):
        return value.astype(jnp.float32)

    def reduce_2(e):
        arrive(f"ry1_{e}", ry1.at[e])
        sy[e] = (f32(gbuf[e, p, :, :, right]) + f32(ry1[e])).astype(jnp.bfloat16)
        for d in (2, 1, 3):
            send(f"ry2_{e}_{d}", sy.at[e, lax.rem(x + d, NX)], ry2.at[e, d - 1], x_peer(d))
        for d in (1, 3, 2):
            arrive(f"rx1_{e}_{d}", rx1.at[e, d - 1])

        def total(q):
            part = f32(gbuf[e, q, x, :, left])
            for d in (1, 2, 3):
                part = part + f32(rx1[e, d - 1, q])
            return part.astype(jnp.bfloat16)

        sx[e, 1] = total(1 - p)
        send(f"rx2_{e}", sx.at[e, 1], rx2.at[e], y_peer)
        sx[e, 0] = total(p)

    act_a, act_b = pl.ds(0, split_hid), pl.ds(split_hid, hid - split_hid)

    def reduce_3(e):
        arrive(f"rx2_{e}", rx2.at[e])
        lower = f32(sx[e, 0]) + f32(rx2[e])
        for d in (1, 3, 2):
            arrive(f"ry2_{e}_{d}", ry2.at[e, d - 1])
        upper = f32(sy[e, x])
        for d in (1, 2, 3):
            upper = upper + f32(ry2[e, d - 1])
        full = jnp.concatenate([lower, upper], axis=1)
        gate, up = full[:, :hid], full[:, hid:]
        hbuf[e, p, x] = (gate / (1.0 + jnp.exp(-gate)) * up).astype(jnp.bfloat16)
        for d in (2, 1, 3):
            send(f"hx1_{e}_{d}", hbuf.at[e, p, x, :, act_a], hbuf.at[e, p, x, :, act_a], x_peer(d))
        send(f"hy1_{e}", hbuf.at[e, p, x, :, act_b], hbuf.at[e, p, x, :, act_b], y_peer)

    def gather_2(e):
        arrive(f"hy1_{e}", hbuf.at[e, 1 - p, x, :, act_b])
        for d in (2, 1, 3):
            send(f"hx2_{e}_{d}", hbuf.at[e, :, x, :, act_b], hbuf.at[e, :, x, :, act_b], x_peer(d))
        for d in (1, 3, 2):
            arrive(f"hx1_{e}_{d}", hbuf.at[e, p, lax.rem(x + NX - d, NX), :, act_a])
        send(f"hy2_{e}", hbuf.at[e, p, :, :, act_a], hbuf.at[e, p, :, :, act_a], y_peer)

    def down(e):
        for d in (1, 3, 2):
            arrive(f"hx2_{e}_{d}", hbuf.at[e, :, lax.rem(x + NX - d, NX), :, act_b])
        arrive(f"hy2_{e}", hbuf.at[e, 1 - p, :, :, act_a])

        def tile(t, carry):
            cols = pl.ds(pl.multiple_of(t * TILE, TILE), TILE)
            part = jnp.dot(
                hbuf[e].reshape(4 * rows, hid),
                w_out[:, cols],
                preferred_element_type=jnp.float32,
            )
            obuf[e, :, :, :, cols] = part.astype(jnp.bfloat16).reshape(2, 2, rows, TILE)
            return carry

        lax.fori_loop(0, width // TILE, tile, 0)
        send(f"oc_{e}", obuf.at[e, 1 - k], rcore.at[e], core_peer)

    def out_2(e):
        arrive(f"oc_{e}", rcore.at[e])
        osum[e] = (f32(obuf[e, k]) + f32(rcore[e])).astype(jnp.bfloat16)
        if e:
            send(f"oz_{e}", osum.at[e], rz.at[e - 1], z_peer(e))

    tiles = both // TILE
    half = tiles // 2
    ready(0)
    w_copies[0].wait()
    w_copies[1].wait()
    e0, e1, e2, e3 = ORDER
    into_gate_up(e0, 0, half)
    forward(e1)
    into_gate_up(e0, half, tiles)
    reduce_1(e0)
    ready(e1)
    into_gate_up(e1, 0, half)
    forward(e2)
    into_gate_up(e1, half, tiles)
    reduce_1(e1)
    reduce_2(e0)
    ready(e2)
    into_gate_up(e2, 0, half)
    forward(e3)
    into_gate_up(e2, half, tiles)
    reduce_1(e2)
    reduce_2(e1)
    reduce_3(e0)
    ready(e3)
    into_gate_up(e3, 0, tiles)
    reduce_1(e3)
    reduce_2(e2)
    reduce_3(e1)
    gather_2(e0)
    reduce_2(e3)
    reduce_3(e2)
    gather_2(e1)
    w_copies[2].wait()
    down(e0)
    reduce_3(e3)
    gather_2(e2)
    down(e1)
    out_2(e0)
    gather_2(e3)
    down(e2)
    out_2(e1)
    down(e3)
    out_2(e2)
    out_2(e3)

    def block(q):
        part = f32(osum[0, q])
        for d in (1, 2, 3):
            part = part + f32(rz[d - 1, q])
        return part

    for d in (1, 3, 2):
        arrive(f"oz_{d}", rz.at[d - 1])
    fpeer[...] = block(1 - s).astype(jnp.bfloat16)
    send("os", fpeer, rside, side_peer)
    mine = block(s)
    arrive("os", rside)
    fin[...] = (mine + f32(rside[...])).astype(jnp.bfloat16)

    back = copy("back", fin, rfin, turn_peer)
    back_here = pltpu.make_async_copy(fin, rfin, loc_sem.at[0])

    @pl.when(diagonal)
    def _():
        back_here.start()
        back_here.wait()

    @pl.when(jnp.logical_not(diagonal))
    def _():
        back.start()
        back.wait()

    out_ref[...] = (f32(res_ref[...]) + f32(rfin[...])).astype(jnp.bfloat16)

    for cp in sent:
        cp.wait_send()

    @pl.when(jnp.logical_not(diagonal))
    def _():
        turn.wait_send()

    for j in range(8):

        @pl.when(jnp.logical_not(jnp.logical_and(diagonal, j == r)))
        def _():
            sq_out[j].wait_send()


def feed_forward(residual, squares, gain, mask, gate_weight, up_weight, down_weight, model):
    rows, width = residual.shape
    hid = gate_weight.shape[1]
    both = 2 * hid
    split_in = both // TILE * 6 // 13 * TILE
    split_hid = hid // 128 * 7 // 13 * 128
    n_copies = 136
    cfg = dict(
        rows=rows,
        width=width,
        hid=hid,
        split_in=split_in,
        split_hid=split_hid,
        model=model,
        sq0=n_copies,
    )
    bf16 = jnp.bfloat16
    rest = both - split_in
    vmem = pl.BlockSpec(memory_space=pltpu.VMEM)
    hbm = pl.BlockSpec(memory_space=pl.ANY)
    scratch = [
        pltpu.VMEM((width, both), bf16),
        pltpu.VMEM((hid, width), bf16),
        pltpu.VMEM((rows, width), bf16),
        pltpu.VMEM((8, 8, 128), jnp.float32),
        pltpu.VMEM((NZ, 2, 2, rows, width), bf16),
        pltpu.VMEM((NZ, 2, NX, STRIPE, both), bf16),
        pltpu.VMEM((NZ, NX - 1, 2, STRIPE, split_in), bf16),
        pltpu.VMEM((NZ, 2, STRIPE, split_in), bf16),
        pltpu.VMEM((NZ, STRIPE, split_in), bf16),
        pltpu.VMEM((NZ, NX, STRIPE, rest), bf16),
        pltpu.VMEM((NZ, NX, STRIPE, rest), bf16),
        pltpu.VMEM((NZ, NX - 1, STRIPE, rest), bf16),
        pltpu.VMEM((NZ, 2, NX, STRIPE, hid), bf16),
        pltpu.VMEM((NZ, 2, 2, rows, width), bf16),
        pltpu.VMEM((NZ, 2, rows, width), bf16),
        pltpu.VMEM((NZ, 2, rows, width), bf16),
        pltpu.VMEM((NZ - 1, 2, rows, width), bf16),
        pltpu.VMEM((rows, width), bf16),
        pltpu.VMEM((rows, width), bf16),
        pltpu.VMEM((rows, width), bf16),
        pltpu.VMEM((rows, width), bf16),
        pltpu.SemaphoreType.DMA((3,)),
        pltpu.SemaphoreType.DMA((n_copies + 8,)),
        pltpu.SemaphoreType.DMA((n_copies + 8,)),
        pltpu.SemaphoreType.DMA((2,)),
    ]
    return pl.pallas_call(
        functools.partial(ffn_kernel, cfg),
        out_shape=jax.ShapeDtypeStruct((rows, width), bf16),
        in_specs=[vmem, vmem, vmem, vmem, hbm, hbm, hbm],
        out_specs=vmem,
        scratch_shapes=scratch,
        compiler_params=pltpu.CompilerParams(
            collective_id=0, has_side_effects=True, vmem_limit_bytes=60 * 2**20
        ),
    )(residual, squares, gain, mask, gate_weight, up_weight, down_weight)


def on_device(
    query_rows,
    key_cache,
    value_cache,
    cache_lengths,
    residual_in,
    norm_gain,
    outlier_index,
    gate_weight,
    up_weight,
    down_weight,
):
    rows_dev, width_dev = query_rows.shape
    cache_len = key_cache.shape[1]
    kv_local = key_cache.shape[2] // HD
    group_size = width_dev // HD // kv_local
    query_part = query_rows.reshape(rows_dev, kv_local, group_size, HD)
    key_part = key_cache.reshape(rows_dev, cache_len, kv_local, HD)
    value_part = value_cache.reshape(rows_dev, cache_len, kv_local, HD)
    scores = jnp.einsum(
        "igqd,itgd->igqt", query_part, key_part, preferred_element_type=jnp.float32
    ) * HD ** (-0.5)
    valid_mask = jnp.arange(cache_len, dtype=jnp.int32)[None, :] < cache_lengths[:, None]
    scores = jnp.where(valid_mask[:, None, None, :], scores, -1e30)
    top_score = jnp.max(scores, axis=-1, keepdims=True)
    expon = jnp.exp(scores - top_score)
    attn_probs = (expon / jnp.sum(expon, axis=-1, keepdims=True)).astype(jnp.bfloat16)
    attention = jnp.einsum(
        "igqt,itgd->igqd", attn_probs, value_part, preferred_element_type=jnp.float32
    ).reshape(rows_dev, width_dev)
    residual = (residual_in.astype(jnp.float32) + attention).astype(jnp.bfloat16)
    squares = jnp.sum(jnp.square(residual.astype(jnp.float32)), axis=1)
    squares = jnp.zeros((8, 128), jnp.float32).at[0, :rows_dev].set(squares)
    slice_width = gate_weight.shape[0]
    first = lax.axis_index("row") * slice_width
    gain = lax.dynamic_slice(norm_gain, (first,), (slice_width,))[None, :]
    channel = first + jnp.arange(slice_width, dtype=jnp.int32)
    mask = jnp.any(channel[:, None] == outlier_index[None, :], axis=1)
    mask = mask.astype(jnp.float32)[None, :]
    return feed_forward(
        residual, squares, gain, mask, gate_weight, up_weight, down_weight, norm_gain.shape[0]
    )


def solution(mesh):
    in_specs = (
        P(("side", "row"), "col"),
        P(("side", "row"), None, "col"),
        P(("side", "row"), None, "col"),
        P(("side", "row")),
        P(("side", "row"), "col"),
        P(),
        P(),
        P("row", ("side", "col")),
        P("row", ("side", "col")),
        P(("side", "col"), "row"),
    )
    out_specs = P(("side", "row"), "col")
    return jax.shard_map(
        on_device, mesh=mesh, in_specs=in_specs, out_specs=out_specs, check_vma=False
    )
```

```python
import functools

import jax
import jax.numpy as jnp
from jax import lax
from jax.experimental import pallas as pl
from jax.experimental.pallas import tpu as pltpu
from jax.sharding import PartitionSpec as P

HD = 128
MESH = pl.DeviceIdType.MESH
STRIPE = 16
TILE = 256
NX = 4
NZ = 4
ORDER = (0, 1, 3, 2)
RING = (0, 1, 3, 2)
PIECES = 2


def ffn_kernel(
    cfg,
    index_ref,
    res_ref,
    gain_hbm,
    gate_hbm,
    up_hbm,
    down_hbm,
    out_ref,
    w_in,
    w_out,
    gain_ref,
    mask_ref,
    sq_ref,
    turned,
    sq_buf,
    xbuf,
    gbuf,
    rx1,
    sx,
    rx2,
    ry1,
    sy,
    ry2,
    fx,
    fy,
    hbuf,
    obuf,
    rcore,
    osum,
    rz,
    fpeer,
    rside,
    fin,
    w_sem,
    send_sem,
    recv_sem,
    loc_sem,
):
    rows, width, hid = cfg["rows"], cfg["width"], cfg["hid"]
    split_in, split_hid = cfg["split_in"], cfg["split_hid"]
    both = 2 * hid
    s, r, c = lax.axis_index("side"), lax.axis_index("row"), lax.axis_index("col")
    x, p = r // 2, lax.rem(r, 2)
    z, k = c // 2, lax.rem(c, 2)
    diagonal = r == c

    def x_peer(d):
        return (s, lax.rem(x + d, NX) * 2 + p, c)

    def z_peer(d):
        return (s, r, lax.rem(z + d, NZ) * 2 + k)

    y_peer = (s, x * 2 + 1 - p, c)
    side_peer = (1 - s, r, c)
    core_peer = (s, r, z * 2 + 1 - k)
    turn_peer = (s, c, r)

    ids = {}

    def copy(name, src, dst, device):
        i = ids.setdefault(name, len(ids))
        return pltpu.make_async_remote_copy(
            src_ref=src,
            dst_ref=dst,
            send_sem=send_sem.at[i],
            recv_sem=recv_sem.at[i],
            device_id=device,
            device_id_type=MESH,
        )

    sent = []

    def send(name, src, dst, device):
        cp = copy(name, src, dst, device)
        cp.start()
        sent.append(cp)

    def arrive(name, dst):
        copy(name, dst, dst, core_peer).wait_recv()

    w_copies = [
        pltpu.make_async_copy(gate_hbm, w_in.at[:, pl.ds(0, hid)], w_sem.at[0]),
        pltpu.make_async_copy(up_hbm, w_in.at[:, pl.ds(hid, hid)], w_sem.at[1]),
        pltpu.make_async_copy(down_hbm, w_out, w_sem.at[2]),
    ]
    gain_copy = pltpu.make_async_copy(
        gain_hbm.at[:, pl.ds(pl.multiple_of(r * width, width), width)], gain_ref, w_sem.at[3]
    )
    gain_copy.start()
    for cp in w_copies:
        cp.start()

    barrier = pltpu.get_barrier_semaphore()
    greet = [x_peer(d) for d in range(1, NX)] + [z_peer(d) for d in range(1, NZ)]
    greet += [y_peer, side_peer, core_peer]
    for device in greet:
        pl.semaphore_signal(barrier, inc=1, device_id=device, device_id_type=MESH)
    for j in range(8):

        @pl.when(jnp.logical_not(jnp.logical_and(diagonal, j == r)))
        def _():
            pl.semaphore_signal(barrier, inc=1, device_id=(s, c, j), device_id_type=MESH)

    eye = lax.broadcasted_iota(jnp.int32, (rows, 128), 0) == lax.broadcasted_iota(
        jnp.int32, (rows, 128), 1
    )
    sq_part = jnp.sum(jnp.square(res_ref[...].astype(jnp.float32)), axis=1, keepdims=True)
    sq_ref[...] = jnp.broadcast_to(
        jnp.sum(jnp.where(eye, sq_part, 0.0), axis=0, keepdims=True), (8, 128)
    )
    pl.semaphore_wait(barrier, len(greet) + 8 - diagonal.astype(jnp.int32))

    def half(h):
        return pl.ds(h * STRIPE, STRIPE)

    turns = [
        copy(f"turn_{h}", res_ref.at[half(h)], turned.at[half(h)], turn_peer) for h in (0, 1)
    ]
    turn_here = pltpu.make_async_copy(res_ref, turned, loc_sem.at[0])
    sq_here = pltpu.make_async_copy(sq_ref, sq_buf.at[c], loc_sem.at[1])

    @pl.when(jnp.logical_not(diagonal))
    def _():
        turns[0].start()

    sq_out = []
    for j in range(8):
        cp = pltpu.make_async_remote_copy(
            src_ref=sq_ref,
            dst_ref=sq_buf.at[c],
            send_sem=send_sem.at[cfg["sq0"] + j],
            recv_sem=recv_sem.at[cfg["sq0"] + c],
            device_id=(s, j, r),
            device_id_type=MESH,
        )
        sq_out.append(cp)

        @pl.when(jnp.logical_not(jnp.logical_and(diagonal, j == r)))
        def _():
            cp.start()

    @pl.when(diagonal)
    def _():
        turn_here.start()
        sq_here.start()
        turn_here.wait()
        sq_here.wait()

    channel = lax.broadcasted_iota(jnp.int32, (1, width), 1) + r * width

    def match(j, found):
        return jnp.where(channel == index_ref[j], 1.0, found)

    mask_ref[...] = lax.fori_loop(
        0, index_ref.shape[0], match, jnp.zeros((1, width), jnp.float32), unroll=8
    )
    gain_copy.wait()

    @pl.when(jnp.logical_not(diagonal))
    def _():
        turns[0].wait_send()
        turns[1].start()

    for j in range(8):

        @pl.when(jnp.logical_not(jnp.logical_and(diagonal, j == c)))
        def _():
            pltpu.make_async_remote_copy(
                src_ref=sq_ref,
                dst_ref=sq_buf.at[j],
                send_sem=send_sem.at[cfg["sq0"] + j],
                recv_sem=recv_sem.at[cfg["sq0"] + j],
                device_id=core_peer,
                device_id_type=MESH,
            ).wait_recv()

    sq_row = jnp.sum(sq_buf[...], axis=0)[0:1, :]
    sq_col = jnp.sum(
        jnp.where(eye, jnp.broadcast_to(sq_row, (rows, 128)), 0.0), axis=1, keepdims=True
    )
    inv = 1.0 / jnp.sqrt(sq_col / cfg["model"] + 1e-5)

    def first(h):
        @pl.when(jnp.logical_not(diagonal))
        def _():
            turns[h].wait_recv()

        normed = turned[half(h)].astype(jnp.float32) * inv[h * STRIPE : (h + 1) * STRIPE]
        normed = normed * gain_ref[...]
        kept = jnp.where(mask_ref[...] > 0.5, normed, jnp.clip(normed, -3.0, 3.0))
        xbuf[2 * h, k, z] = kept.astype(jnp.bfloat16)
        send(f"g_s{h}", xbuf.at[2 * h, k, z], xbuf.at[2 * h + 1, k, z], side_peer)

    def along_z(e):
        for d in (2, 1, 3):
            send(f"g_z{e}_{d}", xbuf.at[e, k, z], xbuf.at[e, k, z], z_peer(d))

    def second(h):
        arrive(f"g_s{h}", xbuf.at[2 * h + 1, k, z])
        along_z(2 * h + 1)

    def forward(e):
        for d in (1, 3, 2):
            arrive(f"g_z{e}_{d}", xbuf.at[e, k, lax.rem(z + NZ - d, NZ)])
        send(f"g_c{e}", xbuf.at[e, k], xbuf.at[e, k], core_peer)

    def ready(e):
        arrive(f"g_c{e}", xbuf.at[e, 1 - k])

    def into_gate_up(e, lo, hi):
        for t in range(lo, hi):
            cols = pl.ds(t * TILE, TILE)
            part = jnp.dot(
                xbuf[e].reshape(4 * rows, width),
                w_in[:, cols],
                preferred_element_type=jnp.float32,
            )
            gbuf[e, :, :, :, cols] = part.astype(jnp.bfloat16).reshape(2, NX, STRIPE, TILE)

    left, right = pl.ds(0, split_in), pl.ds(split_in, both - split_in)

    def f32(value):
        return value.astype(jnp.float32)

    def halves(lo, size):
        mid = size // 256 * 128
        return pl.ds(lo, mid), pl.ds(lo + mid, size - mid)

    up, far, back_x = (lax.rem(x + d, NX) for d in (1, 2, 3))

    def ring_1(tag, src, land, a, b):
        send(tag + "fa", src(far, a), land(2, a), x_peer(1))
        send(tag + "fb", src(far, b), land(2, b), x_peer(3))
        send(tag + "ub", src(up, b), land(0, b), x_peer(1))
        send(tag + "da", src(back_x, a), land(1, a), x_peer(3))

    def ring_2(tag, src, land, stage, a, b):
        arrive(tag + "fa", land(2, a))
        stage(a)[...] = (f32(land(2, a)[...]) + f32(src(up, a)[...])).astype(jnp.bfloat16)
        send(tag + "ua", stage(a), land(0, a), x_peer(1))
        arrive(tag + "fb", land(2, b))
        stage(b)[...] = (f32(land(2, b)[...]) + f32(src(back_x, b)[...])).astype(jnp.bfloat16)
        send(tag + "db", stage(b), land(1, b), x_peer(3))

    def ring_3(tag, land, a, b):
        arrive(tag + "ub", land(0, b))
        arrive(tag + "da", land(1, a))
        arrive(tag + "ua", land(0, a))
        arrive(tag + "db", land(1, b))

    left_a, left_b = halves(0, split_in)
    rest_a, rest_b = halves(0, both - split_in)

    def x_first(e):
        return (
            f"rx1_{e}",
            lambda i, cols: gbuf.at[e, :, i, :, cols],
            lambda slot, cols: rx1.at[e, slot, :, :, cols],
            lambda cols: fx.at[e, :, :, cols],
        )

    def x_second(e):
        return (
            f"ry2_{e}",
            lambda i, cols: sy.at[e, i, :, cols],
            lambda slot, cols: ry2.at[e, slot, :, cols],
            lambda cols: fy.at[e, :, cols],
        )

    def reduce_1x(e):
        if e in RING:
            tag, src, land, _ = x_first(e)
            ring_1(tag, src, land, left_a, left_b)
            return
        for d in (2, 1, 3):
            send(
                f"rx1_{e}_{d}",
                gbuf.at[e, :, lax.rem(x + d, NX), :, left],
                rx1.at[e, d - 1],
                x_peer(d),
            )

    def reduce_1y(e):
        send(f"ry1_{e}", gbuf.at[e, 1 - p, :, :, right], ry1.at[e], y_peer)

    def x_total(e):
        slots = (0, 1) if e in RING else (0, 1, 2)

        def total(q):
            part = f32(gbuf[e, q, x, :, left])
            for slot in slots:
                part = part + f32(rx1[e, slot, q])
            return part.astype(jnp.bfloat16)

        sx[e, 1] = total(1 - p)
        send(f"rx2_{e}", sx.at[e, 1], rx2.at[e], y_peer)
        sx[e, 0] = total(p)

    def reduce_2(e):
        if e in RING:
            tag, src, land, stage = x_first(e)
            ring_2(tag, src, land, stage, left_a, left_b)
        arrive(f"ry1_{e}", ry1.at[e])
        sy[e] = (f32(gbuf[e, p, :, :, right]) + f32(ry1[e])).astype(jnp.bfloat16)
        if e in RING:
            tag, src, land, _ = x_second(e)
            ring_1(tag, src, land, rest_a, rest_b)
            return
        for d in (2, 1, 3):
            send(f"ry2_{e}_{d}", sy.at[e, lax.rem(x + d, NX)], ry2.at[e, d - 1], x_peer(d))
        for d in (1, 3, 2):
            arrive(f"rx1_{e}_{d}", rx1.at[e, d - 1])
        x_total(e)

    def reduce_2b(e):
        if e not in RING:
            return
        tag, _, land, _ = x_first(e)
        ring_3(tag, land, left_a, left_b)
        x_total(e)
        tag, src, land, stage = x_second(e)
        ring_2(tag, src, land, stage, rest_a, rest_b)

    act_a, act_b = pl.ds(0, split_hid), pl.ds(split_hid, hid - split_hid)
    act_aa, act_ab = halves(0, split_hid)
    act_ba, act_bb = halves(split_hid, hid - split_hid)

    def reduce_3(e):
        arrive(f"rx2_{e}", rx2.at[e])
        lower = f32(sx[e, 0]) + f32(rx2[e])
        upper = f32(sy[e, x])
        if e in RING:
            tag, _, land, _ = x_second(e)
            ring_3(tag, land, rest_a, rest_b)
        for d in (1, 2) if e in RING else (1, 2, 3):
            if e not in RING:
                arrive(f"ry2_{e}_{d}", ry2.at[e, d - 1])
            upper = upper + f32(ry2[e, d - 1])
        full = jnp.concatenate([lower, upper], axis=1)
        gate, up_sum = full[:, :hid], full[:, hid:]
        hbuf[e, p, x] = (gate / (1.0 + jnp.exp(-gate)) * up_sum).astype(jnp.bfloat16)
        for d in (1, 3) if e in RING else (2, 1, 3):
            send(f"hx1_{e}_{d}", hbuf.at[e, p, x, :, act_a], hbuf.at[e, p, x, :, act_a], x_peer(d))
        send(f"hy1_{e}", hbuf.at[e, p, x, :, act_b], hbuf.at[e, p, x, :, act_b], y_peer)

    def row_a(e, i, cols):
        return hbuf.at[e, p, i, :, cols]

    def row_b(e, i, cols):
        return hbuf.at[e, :, i, :, cols]

    def pass_on(e, tag, row, whole, a, b):
        arrive(f"{tag}_{e}_1", row(e, back_x, whole))
        send(f"{tag}_{e}_a", row(e, back_x, a), row(e, back_x, a), x_peer(1))
        arrive(f"{tag}_{e}_3", row(e, up, whole))
        send(f"{tag}_{e}_b", row(e, up, b), row(e, up, b), x_peer(3))

    def passed_on(e, tag, row, a, b):
        arrive(f"{tag}_{e}_a", row(e, far, a))
        arrive(f"{tag}_{e}_b", row(e, far, b))

    def gather_2(e):
        if e in RING:
            pass_on(e, "hx1", row_a, act_a, act_aa, act_ab)
        arrive(f"hy1_{e}", hbuf.at[e, 1 - p, x, :, act_b])
        for d in (1, 3) if e in RING else (2, 1, 3):
            send(f"hx2_{e}_{d}", row_b(e, x, act_b), row_b(e, x, act_b), x_peer(d))
        if e in RING:
            return
        for d in (1, 3, 2):
            arrive(f"hx1_{e}_{d}", row_a(e, lax.rem(x + NX - d, NX), act_a))
        send(f"hy2_{e}", hbuf.at[e, p, :, :, act_a], hbuf.at[e, p, :, :, act_a], y_peer)

    def gather_2b(e):
        if e not in RING:
            return
        passed_on(e, "hx1", row_a, act_aa, act_ab)
        send(f"hy2_{e}", hbuf.at[e, p, :, :, act_a], hbuf.at[e, p, :, :, act_a], y_peer)
        pass_on(e, "hx2", row_b, act_b, act_ba, act_bb)

    def down_ready(e):
        if e in RING:
            passed_on(e, "hx2", row_b, act_ba, act_bb)
        else:
            for d in (1, 3, 2):
                arrive(f"hx2_{e}_{d}", row_b(e, lax.rem(x + NX - d, NX), act_b))
        arrive(f"hy2_{e}", hbuf.at[e, 1 - p, :, :, act_a])

    def down_tiles(e, lo, hi):
        for t in range(lo, hi):
            cols = pl.ds(t * TILE, TILE)
            part = jnp.dot(
                hbuf[e].reshape(4 * rows, hid),
                w_out[:, cols],
                preferred_element_type=jnp.float32,
            )
            obuf[e, :, :, :, cols] = part.astype(jnp.bfloat16).reshape(2, NZ, STRIPE, TILE)

    def down(e):
        down_ready(e)
        down_tiles(e, 0, width // TILE)
        send(f"oc_{e}", obuf.at[e, 1 - k], rcore.at[e], core_peer)

    def out_2(e, name, cols):
        arrive(f"oc_{name}", rcore.at[e, :, :, cols])
        osum[e, :, :, cols] = (f32(obuf[e, k, :, :, cols]) + f32(rcore[e, :, :, cols])).astype(
            jnp.bfloat16
        )
        for d in (2, 1, 3):
            send(
                f"oz_{name}_{d}",
                osum.at[e, lax.rem(z + d, NZ), :, cols],
                rz.at[e, d - 1, :, cols],
                z_peer(d),
            )

    def z_sum(e, name, cols):
        part = f32(osum[e, z, :, cols])
        for d in (1, 3, 2):
            arrive(f"oz_{name}_{d}", rz.at[e, d - 1, :, cols])
            part = part + f32(rz[e, d - 1, :, cols])
        return part

    backs = []

    def out_3(e, name, cols):
        h, part = e // 2, z_sum(e, name, cols)
        if e % 2:
            fpeer[half(h), cols] = part.astype(jnp.bfloat16)
            send(f"os_{h}", fpeer.at[half(h), cols], rside.at[half(h), cols], side_peer)
            return
        if all(back_h != h for back_h, _ in backs):
            arrive(f"os_{h}", rside.at[half(h)])
        fin[half(h), cols] = (part + f32(rside[half(h), cols])).astype(jnp.bfloat16)
        back = copy(
            f"back_{name}", fin.at[half(h), cols], out_ref.at[half(h), cols], turn_peer
        )
        backs.append((h, back))

        @pl.when(jnp.logical_not(diagonal))
        def _():
            back.start()

    tiles = both // TILE
    cut = split_in // TILE

    def gate_up(e, then=None):
        ready(e)
        into_gate_up(e, 0, cut)
        reduce_1x(e)
        if then is not None:
            forward(then)
        into_gate_up(e, cut, tiles)
        reduce_1y(e)

    every = pl.ds(0, width)
    first(0)
    along_z(0)
    first(1)
    second(0)
    forward(0)
    w_copies[0].wait()
    w_copies[1].wait()
    ready(0)
    into_gate_up(0, 0, cut)
    reduce_1x(0)
    second(1)
    along_z(2)
    forward(1)
    into_gate_up(0, cut, tiles)
    reduce_1y(0)
    gate_up(1, 3)
    reduce_2(0)
    gate_up(3, 2)
    reduce_2(1)
    reduce_2b(0)
    gate_up(2)
    reduce_2(3)
    reduce_2b(1)
    reduce_3(0)
    reduce_2(2)
    reduce_2b(3)
    reduce_3(1)
    gather_2(0)
    reduce_2b(2)
    reduce_3(3)
    gather_2(1)
    gather_2b(0)
    reduce_3(2)
    gather_2(3)
    gather_2b(1)
    w_copies[2].wait()
    down(0)
    gather_2(2)
    gather_2b(3)
    down(1)
    out_2(0, 0, every)
    gather_2b(2)
    down(3)
    out_2(1, 1, every)
    out_3(1, 1, every)

    piece = width // PIECES
    blocks = [pl.ds(i * piece, piece) for i in range(PIECES)]
    down_ready(2)
    for i, cols in enumerate(blocks):
        down_tiles(2, i * piece // TILE, (i + 1) * piece // TILE)
        send(f"oc_2{i}", obuf.at[2, 1 - k, :, :, cols], rcore.at[2, :, :, cols], core_peer)
        if i == 0:
            out_2(3, 3, every)
    out_3(0, 0, every)
    for i, cols in enumerate(blocks):
        out_2(2, f"2{i}", cols)
        if i == 0:
            out_3(3, 3, every)
    for i, cols in enumerate(blocks):
        out_3(2, f"2{i}", cols)

    @pl.when(diagonal)
    def _():
        out_ref[...] = fin[...]

    for _, back in backs:

        @pl.when(jnp.logical_not(diagonal))
        def _():
            back.wait()

    for cp in sent:
        cp.wait_send()

    @pl.when(jnp.logical_not(diagonal))
    def _():
        turns[1].wait_send()

    for j in range(8):

        @pl.when(jnp.logical_not(jnp.logical_and(diagonal, j == r)))
        def _():
            sq_out[j].wait_send()


def feed_forward(index, residual, gain, gate_weight, up_weight, down_weight):
    rows, width = residual.shape
    hid = gate_weight.shape[1]
    both = 2 * hid
    split_in = both // TILE * 7 // 13 * TILE
    split_hid = hid // 128 * 6 // 13 * 128
    n_copies = 160
    cfg = dict(
        rows=rows,
        width=width,
        hid=hid,
        split_in=split_in,
        split_hid=split_hid,
        model=gain.shape[1],
        sq0=n_copies,
    )
    bf16 = jnp.bfloat16
    rest = both - split_in
    vmem = pl.BlockSpec(memory_space=pltpu.VMEM)
    hbm = pl.BlockSpec(memory_space=pl.ANY)
    scratch = [
        pltpu.VMEM((width, both), bf16),
        pltpu.VMEM((hid, width), bf16),
        pltpu.VMEM((1, width), jnp.float32),
        pltpu.VMEM((1, width), jnp.float32),
        pltpu.VMEM((8, 128), jnp.float32),
        pltpu.VMEM((rows, width), bf16),
        pltpu.VMEM((8, 8, 128), jnp.float32),
        pltpu.VMEM((4, 2, NZ, STRIPE, width), bf16),
        pltpu.VMEM((NZ, 2, NX, STRIPE, both), bf16),
        pltpu.VMEM((NZ, NX - 1, 2, STRIPE, split_in), bf16),
        pltpu.VMEM((NZ, 2, STRIPE, split_in), bf16),
        pltpu.VMEM((NZ, STRIPE, split_in), bf16),
        pltpu.VMEM((NZ, NX, STRIPE, rest), bf16),
        pltpu.VMEM((NZ, NX, STRIPE, rest), bf16),
        pltpu.VMEM((NZ, NX - 1, STRIPE, rest), bf16),
        pltpu.VMEM((NZ, 2, STRIPE, split_in), bf16),
        pltpu.VMEM((NZ, STRIPE, rest), bf16),
        pltpu.VMEM((NZ, 2, NX, STRIPE, hid), bf16),
        pltpu.VMEM((4, 2, NZ, STRIPE, width), bf16),
        pltpu.VMEM((4, NZ, STRIPE, width), bf16),
        pltpu.VMEM((4, NZ, STRIPE, width), bf16),
        pltpu.VMEM((4, NZ - 1, STRIPE, width), bf16),
        pltpu.VMEM((rows, width), bf16),
        pltpu.VMEM((rows, width), bf16),
        pltpu.VMEM((rows, width), bf16),
        pltpu.SemaphoreType.DMA((4,)),
        pltpu.SemaphoreType.DMA((n_copies + 8,)),
        pltpu.SemaphoreType.DMA((n_copies + 8,)),
        pltpu.SemaphoreType.DMA((2,)),
    ]
    return pl.pallas_call(
        functools.partial(ffn_kernel, cfg),
        out_shape=jax.ShapeDtypeStruct((rows, width), bf16),
        in_specs=[pl.BlockSpec(memory_space=pltpu.SMEM), vmem, hbm, hbm, hbm, hbm],
        out_specs=vmem,
        scratch_shapes=scratch,
        compiler_params=pltpu.CompilerParams(
            collective_id=0, has_side_effects=True, vmem_limit_bytes=60 * 2**20
        ),
    )(index, residual, gain, gate_weight, up_weight, down_weight)


def on_device(
    query_rows,
    key_cache,
    value_cache,
    cache_lengths,
    residual_in,
    norm_gain,
    outlier_index,
    gate_weight,
    up_weight,
    down_weight,
):
    rows_dev, width_dev = query_rows.shape
    cache_len = key_cache.shape[1]
    kv_local = key_cache.shape[2] // HD
    group_size = width_dev // HD // kv_local
    query_part = query_rows.reshape(rows_dev, kv_local, group_size, HD)
    key_part = key_cache.reshape(rows_dev, cache_len, kv_local, HD)
    value_part = value_cache.reshape(rows_dev, cache_len, kv_local, HD)
    scores = jnp.einsum(
        "igqd,itgd->igqt", query_part, key_part, preferred_element_type=jnp.float32
    ) * HD ** (-0.5)
    valid_mask = jnp.arange(cache_len, dtype=jnp.int32)[None, :] < cache_lengths[:, None]
    scores = jnp.where(valid_mask[:, None, None, :], scores, -1e30)
    top_score = jnp.max(scores, axis=-1, keepdims=True)
    expon = jnp.exp(scores - top_score)
    attn_probs = (expon / jnp.sum(expon, axis=-1, keepdims=True)).astype(jnp.bfloat16)
    attention = jnp.einsum(
        "igqt,itgd->igqd", attn_probs, value_part, preferred_element_type=jnp.float32
    ).reshape(rows_dev, width_dev)
    residual = (residual_in.astype(jnp.float32) + attention).astype(jnp.bfloat16)
    ffn = feed_forward(
        outlier_index, residual, norm_gain[None, :], gate_weight, up_weight, down_weight
    )
    return (residual.astype(jnp.float32) + ffn.astype(jnp.float32)).astype(jnp.bfloat16)


def solution(mesh):
    in_specs = (
        P(("side", "row"), "col"),
        P(("side", "row"), None, "col"),
        P(("side", "row"), None, "col"),
        P(("side", "row")),
        P(("side", "row"), "col"),
        P(),
        P(),
        P("row", ("side", "col")),
        P("row", ("side", "col")),
        P(("side", "col"), "row"),
    )
    out_specs = P(("side", "row"), "col")
    return jax.shard_map(
        on_device, mesh=mesh, in_specs=in_specs, out_specs=out_specs, check_vma=False
    )
```

```python
import functools

import jax
import jax.numpy as jnp
from jax import lax
from jax.experimental import pallas as pl
from jax.experimental.pallas import tpu as pltpu
from jax.sharding import PartitionSpec as P

HD = 128
MESH = pl.DeviceIdType.MESH
STRIPE = 16
TILE = 256
NX = 4
NZ = 4
ORDER = (0, 1, 3, 2)
RING = (0, 1, 3, 2)
PIECES = 2


def ffn_kernel(
    cfg,
    index_ref,
    res_ref,
    gain_hbm,
    gate_hbm,
    up_hbm,
    down_hbm,
    out_ref,
    w_in,
    w_out,
    gain_ref,
    mask_ref,
    sq_ref,
    turned,
    sq_buf,
    xbuf,
    gbuf,
    rx1,
    sx,
    rx2,
    ry1,
    sy,
    ry2,
    fx,
    fy,
    hbuf,
    obuf,
    rcore,
    osum,
    rz,
    fpeer,
    rside,
    fin,
    w_sem,
    send_sem,
    recv_sem,
    loc_sem,
):
    rows, width, hid = cfg["rows"], cfg["width"], cfg["hid"]
    split_in, split_hid = cfg["split_in"], cfg["split_hid"]
    both = 2 * hid
    s, r, c = lax.axis_index("side"), lax.axis_index("row"), lax.axis_index("col")
    x, p = r // 2, lax.rem(r, 2)
    z, k = c // 2, lax.rem(c, 2)
    diagonal = r == c

    def x_peer(d):
        return (s, lax.rem(x + d, NX) * 2 + p, c)

    def z_peer(d):
        return (s, r, lax.rem(z + d, NZ) * 2 + k)

    y_peer = (s, x * 2 + 1 - p, c)
    side_peer = (1 - s, r, c)
    core_peer = (s, r, z * 2 + 1 - k)
    turn_peer = (s, c, r)

    ids = {}

    def copy(name, src, dst, device):
        i = ids.setdefault(name, len(ids))
        return pltpu.make_async_remote_copy(
            src_ref=src,
            dst_ref=dst,
            send_sem=send_sem.at[i],
            recv_sem=recv_sem.at[i],
            device_id=device,
            device_id_type=MESH,
        )

    sent = []

    def send(name, src, dst, device):
        cp = copy(name, src, dst, device)
        cp.start()
        sent.append(cp)

    def arrive(name, dst):
        copy(name, dst, dst, core_peer).wait_recv()

    w_copies = [
        pltpu.make_async_copy(gate_hbm, w_in.at[:, pl.ds(0, hid)], w_sem.at[0]),
        pltpu.make_async_copy(up_hbm, w_in.at[:, pl.ds(hid, hid)], w_sem.at[1]),
        pltpu.make_async_copy(down_hbm, w_out, w_sem.at[2]),
    ]
    gain_copy = pltpu.make_async_copy(
        gain_hbm.at[:, pl.ds(pl.multiple_of(r * width, width), width)], gain_ref, w_sem.at[3]
    )
    gain_copy.start()
    for cp in w_copies:
        cp.start()

    barrier = pltpu.get_barrier_semaphore()
    greet = [x_peer(d) for d in range(1, NX)] + [z_peer(d) for d in range(1, NZ)]
    greet += [y_peer, side_peer, core_peer]
    for device in greet:
        pl.semaphore_signal(barrier, inc=1, device_id=device, device_id_type=MESH)
    for j in range(8):

        @pl.when(jnp.logical_not(jnp.logical_and(diagonal, j == r)))
        def _():
            pl.semaphore_signal(barrier, inc=1, device_id=(s, c, j), device_id_type=MESH)

    eye = lax.broadcasted_iota(jnp.int32, (rows, 128), 0) == lax.broadcasted_iota(
        jnp.int32, (rows, 128), 1
    )
    sq_part = jnp.sum(jnp.square(res_ref[...].astype(jnp.float32)), axis=1, keepdims=True)
    sq_ref[...] = jnp.broadcast_to(
        jnp.sum(jnp.where(eye, sq_part, 0.0), axis=0, keepdims=True), (8, 128)
    )
    pl.semaphore_wait(barrier, len(greet) + 8 - diagonal.astype(jnp.int32))

    def half(h):
        return pl.ds(h * STRIPE, STRIPE)

    turns = [
        copy(f"turn_{h}", res_ref.at[half(h)], turned.at[half(h)], turn_peer) for h in (0, 1)
    ]
    turn_here = pltpu.make_async_copy(res_ref, turned, loc_sem.at[0])
    sq_here = pltpu.make_async_copy(sq_ref, sq_buf.at[c], loc_sem.at[1])

    @pl.when(jnp.logical_not(diagonal))
    def _():
        turns[0].start()

    sq_out = []
    for j in range(8):
        cp = pltpu.make_async_remote_copy(
            src_ref=sq_ref,
            dst_ref=sq_buf.at[c],
            send_sem=send_sem.at[cfg["sq0"] + j],
            recv_sem=recv_sem.at[cfg["sq0"] + c],
            device_id=(s, j, r),
            device_id_type=MESH,
        )
        sq_out.append(cp)

        @pl.when(jnp.logical_not(jnp.logical_and(diagonal, j == r)))
        def _():
            cp.start()

    @pl.when(diagonal)
    def _():
        turn_here.start()
        sq_here.start()
        turn_here.wait()
        sq_here.wait()

    channel = lax.broadcasted_iota(jnp.int32, (1, width), 1) + r * width

    def match(j, found):
        return jnp.where(channel == index_ref[j], 1.0, found)

    mask_ref[...] = lax.fori_loop(
        0, index_ref.shape[0], match, jnp.zeros((1, width), jnp.float32), unroll=8
    )
    gain_copy.wait()

    @pl.when(jnp.logical_not(diagonal))
    def _():
        turns[0].wait_send()
        turns[1].start()

    for j in range(8):

        @pl.when(jnp.logical_not(jnp.logical_and(diagonal, j == c)))
        def _():
            pltpu.make_async_remote_copy(
                src_ref=sq_ref,
                dst_ref=sq_buf.at[j],
                send_sem=send_sem.at[cfg["sq0"] + j],
                recv_sem=recv_sem.at[cfg["sq0"] + j],
                device_id=core_peer,
                device_id_type=MESH,
            ).wait_recv()

    sq_row = jnp.sum(sq_buf[...], axis=0)[0:1, :]
    sq_col = jnp.sum(
        jnp.where(eye, jnp.broadcast_to(sq_row, (rows, 128)), 0.0), axis=1, keepdims=True
    )
    inv = 1.0 / jnp.sqrt(sq_col / cfg["model"] + 1e-5)

    def first(h):
        @pl.when(jnp.logical_not(diagonal))
        def _():
            turns[h].wait_recv()

        normed = turned[half(h)].astype(jnp.float32) * inv[h * STRIPE : (h + 1) * STRIPE]
        normed = normed * gain_ref[...]
        kept = jnp.where(mask_ref[...] > 0.5, normed, jnp.clip(normed, -3.0, 3.0))
        xbuf[2 * h, k, z] = kept.astype(jnp.bfloat16)
        send(f"g_s{h}", xbuf.at[2 * h, k, z], xbuf.at[2 * h + 1, k, z], side_peer)

    def along_z(e):
        for d in (2, 1, 3):
            send(f"g_z{e}_{d}", xbuf.at[e, k, z], xbuf.at[e, k, z], z_peer(d))

    def second(h):
        arrive(f"g_s{h}", xbuf.at[2 * h + 1, k, z])
        along_z(2 * h + 1)

    def forward(e):
        for d in (1, 3, 2):
            arrive(f"g_z{e}_{d}", xbuf.at[e, k, lax.rem(z + NZ - d, NZ)])
        send(f"g_c{e}", xbuf.at[e, k], xbuf.at[e, k], core_peer)

    def ready(e):
        arrive(f"g_c{e}", xbuf.at[e, 1 - k])

    def into_gate_up(e, lo, hi):
        for t in range(lo, hi):
            cols = pl.ds(t * TILE, TILE)
            part = jnp.dot(
                xbuf[e].reshape(4 * rows, width),
                w_in[:, cols],
                preferred_element_type=jnp.float32,
            )
            gbuf[e, :, :, :, cols] = part.astype(jnp.bfloat16).reshape(2, NX, STRIPE, TILE)

    left, right = pl.ds(0, split_in), pl.ds(split_in, both - split_in)

    def f32(value):
        return value.astype(jnp.float32)

    def halves(lo, size):
        mid = size // 256 * 128
        return pl.ds(lo, mid), pl.ds(lo + mid, size - mid)

    up, far, back_x = (lax.rem(x + d, NX) for d in (1, 2, 3))

    def ring_1(tag, src, land, a, b):
        send(tag + "fa", src(far, a), land(2, a), x_peer(1))
        send(tag + "fb", src(far, b), land(2, b), x_peer(3))
        send(tag + "ub", src(up, b), land(0, b), x_peer(1))
        send(tag + "da", src(back_x, a), land(1, a), x_peer(3))

    def ring_2(tag, src, land, stage, a, b):
        arrive(tag + "fa", land(2, a))
        stage(a)[...] = (f32(land(2, a)[...]) + f32(src(up, a)[...])).astype(jnp.bfloat16)
        send(tag + "ua", stage(a), land(0, a), x_peer(1))
        arrive(tag + "fb", land(2, b))
        stage(b)[...] = (f32(land(2, b)[...]) + f32(src(back_x, b)[...])).astype(jnp.bfloat16)
        send(tag + "db", stage(b), land(1, b), x_peer(3))

    def ring_3(tag, land, a, b):
        arrive(tag + "ub", land(0, b))
        arrive(tag + "da", land(1, a))
        arrive(tag + "ua", land(0, a))
        arrive(tag + "db", land(1, b))

    left_a, left_b = halves(0, split_in)
    rest_a, rest_b = halves(0, both - split_in)

    def x_first(e):
        return (
            f"rx1_{e}",
            lambda i, cols: gbuf.at[e, :, i, :, cols],
            lambda slot, cols: rx1.at[e, slot, :, :, cols],
            lambda cols: fx.at[e, :, :, cols],
        )

    def x_second(e):
        return (
            f"ry2_{e}",
            lambda i, cols: sy.at[e, i, :, cols],
            lambda slot, cols: ry2.at[e, slot, :, cols],
            lambda cols: fy.at[e, :, cols],
        )

    def reduce_1x(e):
        if e in RING:
            tag, src, land, _ = x_first(e)
            ring_1(tag, src, land, left_a, left_b)
            return
        for d in (2, 1, 3):
            send(
                f"rx1_{e}_{d}",
                gbuf.at[e, :, lax.rem(x + d, NX), :, left],
                rx1.at[e, d - 1],
                x_peer(d),
            )

    def reduce_1y(e):
        send(f"ry1_{e}", gbuf.at[e, 1 - p, :, :, right], ry1.at[e], y_peer)

    def x_total(e):
        slots = (0, 1) if e in RING else (0, 1, 2)

        def total(q):
            part = f32(gbuf[e, q, x, :, left])
            for slot in slots:
                part = part + f32(rx1[e, slot, q])
            return part.astype(jnp.bfloat16)

        sx[e, 1] = total(1 - p)
        send(f"rx2_{e}", sx.at[e, 1], rx2.at[e], y_peer)
        sx[e, 0] = total(p)

    def reduce_2(e):
        if e in RING:
            tag, src, land, stage = x_first(e)
            ring_2(tag, src, land, stage, left_a, left_b)
        arrive(f"ry1_{e}", ry1.at[e])
        sy[e] = (f32(gbuf[e, p, :, :, right]) + f32(ry1[e])).astype(jnp.bfloat16)
        if e in RING:
            tag, src, land, _ = x_second(e)
            ring_1(tag, src, land, rest_a, rest_b)
            return
        for d in (2, 1, 3):
            send(f"ry2_{e}_{d}", sy.at[e, lax.rem(x + d, NX)], ry2.at[e, d - 1], x_peer(d))
        for d in (1, 3, 2):
            arrive(f"rx1_{e}_{d}", rx1.at[e, d - 1])
        x_total(e)

    def reduce_2b(e):
        if e not in RING:
            return
        tag, _, land, _ = x_first(e)
        ring_3(tag, land, left_a, left_b)
        x_total(e)
        tag, src, land, stage = x_second(e)
        ring_2(tag, src, land, stage, rest_a, rest_b)

    act_a, act_b = pl.ds(0, split_hid), pl.ds(split_hid, hid - split_hid)
    act_aa, act_ab = halves(0, split_hid)
    act_ba, act_bb = halves(split_hid, hid - split_hid)

    def reduce_3(e):
        arrive(f"rx2_{e}", rx2.at[e])
        lower = f32(sx[e, 0]) + f32(rx2[e])
        upper = f32(sy[e, x])
        if e in RING:
            tag, _, land, _ = x_second(e)
            ring_3(tag, land, rest_a, rest_b)
        for d in (1, 2) if e in RING else (1, 2, 3):
            if e not in RING:
                arrive(f"ry2_{e}_{d}", ry2.at[e, d - 1])
            upper = upper + f32(ry2[e, d - 1])
        full = jnp.concatenate([lower, upper], axis=1)
        gate, up_sum = full[:, :hid], full[:, hid:]
        hbuf[e, p, x] = (gate / (1.0 + jnp.exp(-gate)) * up_sum).astype(jnp.bfloat16)
        for d in (1, 3) if e in RING else (2, 1, 3):
            send(f"hx1_{e}_{d}", hbuf.at[e, p, x, :, act_a], hbuf.at[e, p, x, :, act_a], x_peer(d))
        send(f"hy1_{e}", hbuf.at[e, p, x, :, act_b], hbuf.at[e, p, x, :, act_b], y_peer)

    def row_a(e, i, cols):
        return hbuf.at[e, p, i, :, cols]

    def row_b(e, i, cols):
        return hbuf.at[e, :, i, :, cols]

    def pass_on(e, tag, row, whole, a, b):
        arrive(f"{tag}_{e}_1", row(e, back_x, whole))
        send(f"{tag}_{e}_a", row(e, back_x, a), row(e, back_x, a), x_peer(1))
        arrive(f"{tag}_{e}_3", row(e, up, whole))
        send(f"{tag}_{e}_b", row(e, up, b), row(e, up, b), x_peer(3))

    def passed_on(e, tag, row, a, b):
        arrive(f"{tag}_{e}_a", row(e, far, a))
        arrive(f"{tag}_{e}_b", row(e, far, b))

    def gather_2(e):
        if e in RING:
            pass_on(e, "hx1", row_a, act_a, act_aa, act_ab)
        arrive(f"hy1_{e}", hbuf.at[e, 1 - p, x, :, act_b])
        for d in (1, 3) if e in RING else (2, 1, 3):
            send(f"hx2_{e}_{d}", row_b(e, x, act_b), row_b(e, x, act_b), x_peer(d))
        if e in RING:
            return
        for d in (1, 3, 2):
            arrive(f"hx1_{e}_{d}", row_a(e, lax.rem(x + NX - d, NX), act_a))
        send(f"hy2_{e}", hbuf.at[e, p, :, :, act_a], hbuf.at[e, p, :, :, act_a], y_peer)

    def gather_2b(e):
        if e not in RING:
            return
        passed_on(e, "hx1", row_a, act_aa, act_ab)
        send(f"hy2_{e}", hbuf.at[e, p, :, :, act_a], hbuf.at[e, p, :, :, act_a], y_peer)
        pass_on(e, "hx2", row_b, act_b, act_ba, act_bb)

    def down_ready(e):
        if e in RING:
            passed_on(e, "hx2", row_b, act_ba, act_bb)
        else:
            for d in (1, 3, 2):
                arrive(f"hx2_{e}_{d}", row_b(e, lax.rem(x + NX - d, NX), act_b))
        arrive(f"hy2_{e}", hbuf.at[e, 1 - p, :, :, act_a])

    def down_tiles(e, lo, hi):
        for t in range(lo, hi):
            cols = pl.ds(t * TILE, TILE)
            part = jnp.dot(
                hbuf[e].reshape(4 * rows, hid),
                w_out[:, cols],
                preferred_element_type=jnp.float32,
            )
            obuf[e, :, :, :, cols] = part.astype(jnp.bfloat16).reshape(2, NZ, STRIPE, TILE)

    def down(e):
        down_ready(e)
        down_tiles(e, 0, width // TILE)
        send(f"oc_{e}", obuf.at[e, 1 - k], rcore.at[e], core_peer)

    def out_2(e, name, cols):
        arrive(f"oc_{name}", rcore.at[e, :, :, cols])
        osum[e, :, :, cols] = (f32(obuf[e, k, :, :, cols]) + f32(rcore[e, :, :, cols])).astype(
            jnp.bfloat16
        )
        for d in (2, 1, 3):
            send(
                f"oz_{name}_{d}",
                osum.at[e, lax.rem(z + d, NZ), :, cols],
                rz.at[e, d - 1, :, cols],
                z_peer(d),
            )

    def z_sum(e, name, cols):
        part = f32(osum[e, z, :, cols])
        for d in (1, 3, 2):
            arrive(f"oz_{name}_{d}", rz.at[e, d - 1, :, cols])
            part = part + f32(rz[e, d - 1, :, cols])
        return part

    backs = []

    def out_3(e, name, cols):
        h, part = e // 2, z_sum(e, name, cols)
        if e % 2:
            fpeer[half(h), cols] = part.astype(jnp.bfloat16)
            send(f"os_{h}", fpeer.at[half(h), cols], rside.at[half(h), cols], side_peer)
            return
        if all(back_h != h for back_h, _ in backs):
            arrive(f"os_{h}", rside.at[half(h)])
        fin[half(h), cols] = (part + f32(rside[half(h), cols])).astype(jnp.bfloat16)
        back = copy(
            f"back_{name}", fin.at[half(h), cols], out_ref.at[half(h), cols], turn_peer
        )
        backs.append((h, back))

        @pl.when(jnp.logical_not(diagonal))
        def _():
            back.start()

    tiles = both // TILE
    cut = split_in // TILE

    def gate_up(e, then=None):
        ready(e)
        into_gate_up(e, 0, cut)
        reduce_1x(e)
        into_gate_up(e, cut, tiles)
        reduce_1y(e)
        if then is not None:
            forward(then)

    every = pl.ds(0, width)
    first(0)
    along_z(0)
    first(1)
    second(0)
    forward(0)
    w_copies[0].wait()
    w_copies[1].wait()
    ready(0)
    into_gate_up(0, 0, cut)
    reduce_1x(0)
    into_gate_up(0, cut, tiles)
    reduce_1y(0)
    second(1)
    forward(1)
    along_z(2)
    gate_up(1)
    reduce_2(0)
    forward(3)
    gate_up(3)
    reduce_2(1)
    reduce_2b(0)
    forward(2)
    gate_up(2)
    reduce_2(3)
    reduce_2b(1)
    reduce_3(0)
    reduce_2(2)
    reduce_2b(3)
    reduce_3(1)
    gather_2(0)
    reduce_2b(2)
    reduce_3(3)
    gather_2(1)
    gather_2b(0)
    reduce_3(2)
    gather_2(3)
    gather_2b(1)
    gather_2(2)
    gather_2b(3)
    w_copies[2].wait()
    down(0)
    down(1)
    gather_2b(2)
    out_2(0, 0, every)
    down(3)
    out_2(1, 1, every)

    piece = width // PIECES
    blocks = [pl.ds(i * piece, piece) for i in range(PIECES)]
    down_ready(2)
    for i, cols in enumerate(blocks):
        down_tiles(2, i * piece // TILE, (i + 1) * piece // TILE)
        send(f"oc_2{i}", obuf.at[2, 1 - k, :, :, cols], rcore.at[2, :, :, cols], core_peer)
        if i == 0:
            out_2(3, 3, every)
    for i, cols in enumerate(blocks):
        out_2(2, f"2{i}", cols)
        if i == 0:
            out_3(1, 1, every)
    out_3(3, 3, every)
    out_3(0, 0, every)
    for i, cols in enumerate(blocks):
        out_3(2, f"2{i}", cols)

    @pl.when(diagonal)
    def _():
        out_ref[...] = fin[...]

    for _, back in backs:

        @pl.when(jnp.logical_not(diagonal))
        def _():
            back.wait()

    for cp in sent:
        cp.wait_send()

    @pl.when(jnp.logical_not(diagonal))
    def _():
        turns[1].wait_send()

    for j in range(8):

        @pl.when(jnp.logical_not(jnp.logical_and(diagonal, j == r)))
        def _():
            sq_out[j].wait_send()


def feed_forward(index, residual, gain, gate_weight, up_weight, down_weight):
    rows, width = residual.shape
    hid = gate_weight.shape[1]
    both = 2 * hid
    split_in = both // TILE * 7 // 13 * TILE
    split_hid = hid // 128 * 6 // 13 * 128
    n_copies = 160
    cfg = dict(
        rows=rows,
        width=width,
        hid=hid,
        split_in=split_in,
        split_hid=split_hid,
        model=gain.shape[1],
        sq0=n_copies,
    )
    bf16 = jnp.bfloat16
    rest = both - split_in
    vmem = pl.BlockSpec(memory_space=pltpu.VMEM)
    hbm = pl.BlockSpec(memory_space=pl.ANY)
    scratch = [
        pltpu.VMEM((width, both), bf16),
        pltpu.VMEM((hid, width), bf16),
        pltpu.VMEM((1, width), jnp.float32),
        pltpu.VMEM((1, width), jnp.float32),
        pltpu.VMEM((8, 128), jnp.float32),
        pltpu.VMEM((rows, width), bf16),
        pltpu.VMEM((8, 8, 128), jnp.float32),
        pltpu.VMEM((4, 2, NZ, STRIPE, width), bf16),
        pltpu.VMEM((NZ, 2, NX, STRIPE, both), bf16),
        pltpu.VMEM((NZ, NX - 1, 2, STRIPE, split_in), bf16),
        pltpu.VMEM((NZ, 2, STRIPE, split_in), bf16),
        pltpu.VMEM((NZ, STRIPE, split_in), bf16),
        pltpu.VMEM((NZ, NX, STRIPE, rest), bf16),
        pltpu.VMEM((NZ, NX, STRIPE, rest), bf16),
        pltpu.VMEM((NZ, NX - 1, STRIPE, rest), bf16),
        pltpu.VMEM((NZ, 2, STRIPE, split_in), bf16),
        pltpu.VMEM((NZ, STRIPE, rest), bf16),
        pltpu.VMEM((NZ, 2, NX, STRIPE, hid), bf16),
        pltpu.VMEM((4, 2, NZ, STRIPE, width), bf16),
        pltpu.VMEM((4, NZ, STRIPE, width), bf16),
        pltpu.VMEM((4, NZ, STRIPE, width), bf16),
        pltpu.VMEM((4, NZ - 1, STRIPE, width), bf16),
        pltpu.VMEM((rows, width), bf16),
        pltpu.VMEM((rows, width), bf16),
        pltpu.VMEM((rows, width), bf16),
        pltpu.SemaphoreType.DMA((4,)),
        pltpu.SemaphoreType.DMA((n_copies + 8,)),
        pltpu.SemaphoreType.DMA((n_copies + 8,)),
        pltpu.SemaphoreType.DMA((2,)),
    ]
    return pl.pallas_call(
        functools.partial(ffn_kernel, cfg),
        out_shape=jax.ShapeDtypeStruct((rows, width), bf16),
        in_specs=[pl.BlockSpec(memory_space=pltpu.SMEM), vmem, hbm, hbm, hbm, hbm],
        out_specs=vmem,
        scratch_shapes=scratch,
        compiler_params=pltpu.CompilerParams(
            collective_id=0, has_side_effects=True, vmem_limit_bytes=60 * 2**20
        ),
    )(index, residual, gain, gate_weight, up_weight, down_weight)


def on_device(
    query_rows,
    key_cache,
    value_cache,
    cache_lengths,
    residual_in,
    norm_gain,
    outlier_index,
    gate_weight,
    up_weight,
    down_weight,
):
    rows_dev, width_dev = query_rows.shape
    cache_len = key_cache.shape[1]
    kv_local = key_cache.shape[2] // HD
    group_size = width_dev // HD // kv_local
    query_part = query_rows.reshape(rows_dev, kv_local, group_size, HD)
    key_part = key_cache.reshape(rows_dev, cache_len, kv_local, HD)
    value_part = value_cache.reshape(rows_dev, cache_len, kv_local, HD)
    scores = jnp.einsum(
        "igqd,itgd->igqt", query_part, key_part, preferred_element_type=jnp.float32
    ) * HD ** (-0.5)
    valid_mask = jnp.arange(cache_len, dtype=jnp.int32)[None, :] < cache_lengths[:, None]
    scores = jnp.where(valid_mask[:, None, None, :], scores, -1e30)
    top_score = jnp.max(scores, axis=-1, keepdims=True)
    expon = jnp.exp(scores - top_score)
    attn_probs = (expon / jnp.sum(expon, axis=-1, keepdims=True)).astype(jnp.bfloat16)
    attention = jnp.einsum(
        "igqt,itgd->igqd", attn_probs, value_part, preferred_element_type=jnp.float32
    ).reshape(rows_dev, width_dev)
    residual = (residual_in.astype(jnp.float32) + attention).astype(jnp.bfloat16)
    ffn = feed_forward(
        outlier_index, residual, norm_gain[None, :], gate_weight, up_weight, down_weight
    )
    return (residual.astype(jnp.float32) + ffn.astype(jnp.float32)).astype(jnp.bfloat16)


def solution(mesh):
    in_specs = (
        P(("side", "row"), "col"),
        P(("side", "row"), None, "col"),
        P(("side", "row"), None, "col"),
        P(("side", "row")),
        P(("side", "row"), "col"),
        P(),
        P(),
        P("row", ("side", "col")),
        P("row", ("side", "col")),
        P(("side", "col"), "row"),
    )
    out_specs = P(("side", "row"), "col")
    return jax.shard_map(
        on_device, mesh=mesh, in_specs=in_specs, out_specs=out_specs, check_vma=False
    )
```

```python
import functools

import jax
import jax.numpy as jnp
from jax import lax
from jax.experimental import pallas as pl
from jax.experimental.pallas import tpu as pltpu
from jax.sharding import PartitionSpec as P

HD = 128
MESH = pl.DeviceIdType.MESH
STRIPE = 16
TILE = 256
NX = 4
NZ = 4
ORDER = (0, 1, 3, 2)
RING = (0, 1, 3, 2)
PIECES = 2


def ffn_kernel(
    cfg,
    index_ref,
    res_ref,
    gain_hbm,
    gate_hbm,
    up_hbm,
    down_hbm,
    out_ref,
    w_in,
    w_out,
    gain_ref,
    mask_ref,
    sq_ref,
    turned,
    sq_buf,
    xbuf,
    gbuf,
    rx1,
    sx,
    rx2,
    ry1,
    sy,
    ry2,
    fx,
    fy,
    hbuf,
    obuf,
    rcore,
    osum,
    rz,
    fpeer,
    rside,
    fin,
    w_sem,
    send_sem,
    recv_sem,
    loc_sem,
):
    rows, width, hid = cfg["rows"], cfg["width"], cfg["hid"]
    split_in, split_hid = cfg["split_in"], cfg["split_hid"]
    both = 2 * hid
    s, r, c = lax.axis_index("side"), lax.axis_index("row"), lax.axis_index("col")
    x, p = r // 2, lax.rem(r, 2)
    z, k = c // 2, lax.rem(c, 2)
    diagonal = r == c

    def x_peer(d):
        return (s, lax.rem(x + d, NX) * 2 + p, c)

    def z_peer(d):
        return (s, r, lax.rem(z + d, NZ) * 2 + k)

    y_peer = (s, x * 2 + 1 - p, c)
    side_peer = (1 - s, r, c)
    core_peer = (s, r, z * 2 + 1 - k)
    turn_peer = (s, c, r)

    ids = {}

    def copy(name, src, dst, device):
        i = ids.setdefault(name, len(ids))
        return pltpu.make_async_remote_copy(
            src_ref=src,
            dst_ref=dst,
            send_sem=send_sem.at[i],
            recv_sem=recv_sem.at[i],
            device_id=device,
            device_id_type=MESH,
        )

    sent = []

    def send(name, src, dst, device):
        cp = copy(name, src, dst, device)
        cp.start()
        sent.append(cp)

    def arrive(name, dst):
        copy(name, dst, dst, core_peer).wait_recv()

    w_copies = [
        pltpu.make_async_copy(gate_hbm, w_in.at[:, pl.ds(0, hid)], w_sem.at[0]),
        pltpu.make_async_copy(up_hbm, w_in.at[:, pl.ds(hid, hid)], w_sem.at[1]),
        pltpu.make_async_copy(down_hbm, w_out, w_sem.at[2]),
    ]
    gain_copy = pltpu.make_async_copy(
        gain_hbm.at[:, pl.ds(pl.multiple_of(r * width, width), width)], gain_ref, w_sem.at[3]
    )
    gain_copy.start()
    for cp in w_copies:
        cp.start()

    barrier = pltpu.get_barrier_semaphore()
    greet = [x_peer(d) for d in range(1, NX)] + [z_peer(d) for d in range(1, NZ)]
    greet += [y_peer, side_peer, core_peer]
    for device in greet:
        pl.semaphore_signal(barrier, inc=1, device_id=device, device_id_type=MESH)
    for j in range(8):

        @pl.when(jnp.logical_not(jnp.logical_and(diagonal, j == r)))
        def _():
            pl.semaphore_signal(barrier, inc=1, device_id=(s, c, j), device_id_type=MESH)

    eye = lax.broadcasted_iota(jnp.int32, (rows, 128), 0) == lax.broadcasted_iota(
        jnp.int32, (rows, 128), 1
    )
    sq_part = jnp.sum(jnp.square(res_ref[...].astype(jnp.float32)), axis=1, keepdims=True)
    sq_ref[...] = jnp.broadcast_to(
        jnp.sum(jnp.where(eye, sq_part, 0.0), axis=0, keepdims=True), (8, 128)
    )
    pl.semaphore_wait(barrier, len(greet) + 8 - diagonal.astype(jnp.int32))

    def half(h):
        return pl.ds(h * STRIPE, STRIPE)

    turns = [
        copy(f"turn_{h}", res_ref.at[half(h)], turned.at[half(h)], turn_peer) for h in (0, 1)
    ]
    turn_here = pltpu.make_async_copy(res_ref, turned, loc_sem.at[0])
    sq_here = pltpu.make_async_copy(sq_ref, sq_buf.at[c], loc_sem.at[1])

    @pl.when(jnp.logical_not(diagonal))
    def _():
        turns[0].start()

    sq_out = []
    for j in range(8):
        cp = pltpu.make_async_remote_copy(
            src_ref=sq_ref,
            dst_ref=sq_buf.at[c],
            send_sem=send_sem.at[cfg["sq0"] + j],
            recv_sem=recv_sem.at[cfg["sq0"] + c],
            device_id=(s, j, r),
            device_id_type=MESH,
        )
        sq_out.append(cp)

        @pl.when(jnp.logical_not(jnp.logical_and(diagonal, j == r)))
        def _():
            cp.start()

    @pl.when(diagonal)
    def _():
        turn_here.start()
        sq_here.start()
        turn_here.wait()
        sq_here.wait()

    channel = lax.broadcasted_iota(jnp.int32, (1, width), 1) + r * width

    def match(j, found):
        return jnp.where(channel == index_ref[j], 1.0, found)

    mask_ref[...] = lax.fori_loop(
        0, index_ref.shape[0], match, jnp.zeros((1, width), jnp.float32), unroll=8
    )
    gain_copy.wait()

    @pl.when(jnp.logical_not(diagonal))
    def _():
        turns[0].wait_send()
        turns[1].start()

    for j in range(8):

        @pl.when(jnp.logical_not(jnp.logical_and(diagonal, j == c)))
        def _():
            pltpu.make_async_remote_copy(
                src_ref=sq_ref,
                dst_ref=sq_buf.at[j],
                send_sem=send_sem.at[cfg["sq0"] + j],
                recv_sem=recv_sem.at[cfg["sq0"] + j],
                device_id=core_peer,
                device_id_type=MESH,
            ).wait_recv()

    sq_row = jnp.sum(sq_buf[...], axis=0)[0:1, :]
    sq_col = jnp.sum(
        jnp.where(eye, jnp.broadcast_to(sq_row, (rows, 128)), 0.0), axis=1, keepdims=True
    )
    inv = 1.0 / jnp.sqrt(sq_col / cfg["model"] + 1e-5)

    def first(h):
        @pl.when(jnp.logical_not(diagonal))
        def _():
            turns[h].wait_recv()

        normed = turned[half(h)].astype(jnp.float32) * inv[h * STRIPE : (h + 1) * STRIPE]
        normed = normed * gain_ref[...]
        kept = jnp.where(mask_ref[...] > 0.5, normed, jnp.clip(normed, -3.0, 3.0))
        xbuf[2 * h, k, z] = kept.astype(jnp.bfloat16)
        send(f"g_s{h}", xbuf.at[2 * h, k, z], xbuf.at[2 * h + 1, k, z], side_peer)

    def along_z(e):
        for d in (1, 3, 2):
            send(f"g_z{e}_{d}", xbuf.at[e, k, z], xbuf.at[e, k, z], z_peer(d))

    def second(h):
        arrive(f"g_s{h}", xbuf.at[2 * h + 1, k, z])
        along_z(2 * h + 1)

    def forward(e):
        for d in (1, 3, 2):
            arrive(f"g_z{e}_{d}", xbuf.at[e, k, lax.rem(z + NZ - d, NZ)])
        send(f"g_c{e}", xbuf.at[e, k], xbuf.at[e, k], core_peer)

    def ready(e):
        arrive(f"g_c{e}", xbuf.at[e, 1 - k])

    def into_gate_up(e, lo, hi):
        for t in range(lo, hi):
            cols = pl.ds(t * TILE, TILE)
            part = jnp.dot(
                xbuf[e].reshape(4 * rows, width),
                w_in[:, cols],
                preferred_element_type=jnp.float32,
            )
            gbuf[e, :, :, :, cols] = part.astype(jnp.bfloat16).reshape(2, NX, STRIPE, TILE)

    left, right = pl.ds(0, split_in), pl.ds(split_in, both - split_in)

    def f32(value):
        return value.astype(jnp.float32)

    def halves(lo, size):
        mid = size // 256 * 128
        return pl.ds(lo, mid), pl.ds(lo + mid, size - mid)

    up, far, back_x = (lax.rem(x + d, NX) for d in (1, 2, 3))

    def ring_1(tag, src, land, a, b):
        send(tag + "fa", src(far, a), land(2, a), x_peer(1))
        send(tag + "fb", src(far, b), land(2, b), x_peer(3))
        send(tag + "ub", src(up, b), land(0, b), x_peer(1))
        send(tag + "da", src(back_x, a), land(1, a), x_peer(3))

    def ring_2(tag, src, land, stage, a, b):
        arrive(tag + "fa", land(2, a))
        stage(a)[...] = (f32(land(2, a)[...]) + f32(src(up, a)[...])).astype(jnp.bfloat16)
        send(tag + "ua", stage(a), land(0, a), x_peer(1))
        arrive(tag + "fb", land(2, b))
        stage(b)[...] = (f32(land(2, b)[...]) + f32(src(back_x, b)[...])).astype(jnp.bfloat16)
        send(tag + "db", stage(b), land(1, b), x_peer(3))

    def ring_3(tag, land, a, b):
        arrive(tag + "ub", land(0, b))
        arrive(tag + "da", land(1, a))
        arrive(tag + "ua", land(0, a))
        arrive(tag + "db", land(1, b))

    left_a, left_b = halves(0, split_in)
    rest_a, rest_b = halves(0, both - split_in)

    def x_first(e):
        return (
            f"rx1_{e}",
            lambda i, cols: gbuf.at[e, :, i, :, cols],
            lambda slot, cols: rx1.at[e, slot, :, :, cols],
            lambda cols: fx.at[e, :, :, cols],
        )

    def x_second(e):
        return (
            f"ry2_{e}",
            lambda i, cols: sy.at[e, i, :, cols],
            lambda slot, cols: ry2.at[e, slot, :, cols],
            lambda cols: fy.at[e, :, cols],
        )

    def reduce_1x(e):
        if e in RING:
            tag, src, land, _ = x_first(e)
            ring_1(tag, src, land, left_a, left_b)
            return
        for d in (2, 1, 3):
            send(
                f"rx1_{e}_{d}",
                gbuf.at[e, :, lax.rem(x + d, NX), :, left],
                rx1.at[e, d - 1],
                x_peer(d),
            )

    def reduce_1y(e):
        send(f"ry1_{e}", gbuf.at[e, 1 - p, :, :, right], ry1.at[e], y_peer)

    def x_total(e):
        slots = (0, 1) if e in RING else (0, 1, 2)

        def total(q):
            part = f32(gbuf[e, q, x, :, left])
            for slot in slots:
                part = part + f32(rx1[e, slot, q])
            return part.astype(jnp.bfloat16)

        sx[e, 1] = total(1 - p)
        send(f"rx2_{e}", sx.at[e, 1], rx2.at[e], y_peer)
        sx[e, 0] = total(p)

    def reduce_2(e):
        if e in RING:
            tag, src, land, stage = x_first(e)
            ring_2(tag, src, land, stage, left_a, left_b)
        arrive(f"ry1_{e}", ry1.at[e])
        sy[e] = (f32(gbuf[e, p, :, :, right]) + f32(ry1[e])).astype(jnp.bfloat16)
        if e in RING:
            tag, src, land, _ = x_second(e)
            ring_1(tag, src, land, rest_a, rest_b)
            return
        for d in (2, 1, 3):
            send(f"ry2_{e}_{d}", sy.at[e, lax.rem(x + d, NX)], ry2.at[e, d - 1], x_peer(d))
        for d in (1, 3, 2):
            arrive(f"rx1_{e}_{d}", rx1.at[e, d - 1])
        x_total(e)

    def reduce_2b(e):
        if e not in RING:
            return
        tag, _, land, _ = x_first(e)
        ring_3(tag, land, left_a, left_b)
        x_total(e)
        tag, src, land, stage = x_second(e)
        ring_2(tag, src, land, stage, rest_a, rest_b)

    act_a, act_b = pl.ds(0, split_hid), pl.ds(split_hid, hid - split_hid)
    act_aa, act_ab = halves(0, split_hid)
    act_ba, act_bb = halves(split_hid, hid - split_hid)

    def reduce_3(e):
        arrive(f"rx2_{e}", rx2.at[e])
        lower = f32(sx[e, 0]) + f32(rx2[e])
        upper = f32(sy[e, x])
        if e in RING:
            tag, _, land, _ = x_second(e)
            ring_3(tag, land, rest_a, rest_b)
        for d in (1, 2) if e in RING else (1, 2, 3):
            if e not in RING:
                arrive(f"ry2_{e}_{d}", ry2.at[e, d - 1])
            upper = upper + f32(ry2[e, d - 1])
        full = jnp.concatenate([lower, upper], axis=1)
        gate, up_sum = full[:, :hid], full[:, hid:]
        hbuf[e, p, x] = (gate / (1.0 + jnp.exp(-gate)) * up_sum).astype(jnp.bfloat16)
        for d in (1, 3) if e in RING else (2, 1, 3):
            send(f"hx1_{e}_{d}", hbuf.at[e, p, x, :, act_a], hbuf.at[e, p, x, :, act_a], x_peer(d))
        send(f"hy1_{e}", hbuf.at[e, p, x, :, act_b], hbuf.at[e, p, x, :, act_b], y_peer)

    def row_a(e, i, cols):
        return hbuf.at[e, p, i, :, cols]

    def row_b(e, i, cols):
        return hbuf.at[e, :, i, :, cols]

    def pass_on(e, tag, row, whole, a, b):
        arrive(f"{tag}_{e}_1", row(e, back_x, whole))
        send(f"{tag}_{e}_a", row(e, back_x, a), row(e, back_x, a), x_peer(1))
        arrive(f"{tag}_{e}_3", row(e, up, whole))
        send(f"{tag}_{e}_b", row(e, up, b), row(e, up, b), x_peer(3))

    def passed_on(e, tag, row, a, b):
        arrive(f"{tag}_{e}_a", row(e, far, a))
        arrive(f"{tag}_{e}_b", row(e, far, b))

    def gather_2(e):
        if e in RING:
            pass_on(e, "hx1", row_a, act_a, act_aa, act_ab)
        arrive(f"hy1_{e}", hbuf.at[e, 1 - p, x, :, act_b])
        for d in (1, 3) if e in RING else (2, 1, 3):
            send(f"hx2_{e}_{d}", row_b(e, x, act_b), row_b(e, x, act_b), x_peer(d))
        if e in RING:
            return
        for d in (1, 3, 2):
            arrive(f"hx1_{e}_{d}", row_a(e, lax.rem(x + NX - d, NX), act_a))
        send(f"hy2_{e}", hbuf.at[e, p, :, :, act_a], hbuf.at[e, p, :, :, act_a], y_peer)

    def gather_2b(e):
        if e not in RING:
            return
        passed_on(e, "hx1", row_a, act_aa, act_ab)
        send(f"hy2_{e}", hbuf.at[e, p, :, :, act_a], hbuf.at[e, p, :, :, act_a], y_peer)
        pass_on(e, "hx2", row_b, act_b, act_ba, act_bb)

    def down_ready(e):
        if e in RING:
            passed_on(e, "hx2", row_b, act_ba, act_bb)
        else:
            for d in (1, 3, 2):
                arrive(f"hx2_{e}_{d}", row_b(e, lax.rem(x + NX - d, NX), act_b))
        arrive(f"hy2_{e}", hbuf.at[e, 1 - p, :, :, act_a])

    def down_tiles(e, lo, hi):
        for t in range(lo, hi):
            cols = pl.ds(t * TILE, TILE)
            part = jnp.dot(
                hbuf[e].reshape(4 * rows, hid),
                w_out[:, cols],
                preferred_element_type=jnp.float32,
            )
            obuf[e, :, :, :, cols] = part.astype(jnp.bfloat16).reshape(2, NZ, STRIPE, TILE)

    def down(e):
        down_ready(e)
        down_tiles(e, 0, width // TILE)
        send(f"oc_{e}", obuf.at[e, 1 - k], rcore.at[e], core_peer)

    def out_2(e, name, cols):
        arrive(f"oc_{name}", rcore.at[e, :, :, cols])
        osum[e, :, :, cols] = (f32(obuf[e, k, :, :, cols]) + f32(rcore[e, :, :, cols])).astype(
            jnp.bfloat16
        )
        for d in (2, 1, 3):
            send(
                f"oz_{name}_{d}",
                osum.at[e, lax.rem(z + d, NZ), :, cols],
                rz.at[e, d - 1, :, cols],
                z_peer(d),
            )

    def z_sum(e, name, cols):
        part = f32(osum[e, z, :, cols])
        for d in (1, 3, 2):
            arrive(f"oz_{name}_{d}", rz.at[e, d - 1, :, cols])
            part = part + f32(rz[e, d - 1, :, cols])
        return part

    backs = []

    def out_3(e, name, cols):
        h, part = e // 2, z_sum(e, name, cols)
        if e % 2:
            fpeer[half(h), cols] = part.astype(jnp.bfloat16)
            send(f"os_{h}", fpeer.at[half(h), cols], rside.at[half(h), cols], side_peer)
            return
        if all(back_h != h for back_h, _ in backs):
            arrive(f"os_{h}", rside.at[half(h)])
        fin[half(h), cols] = (part + f32(rside[half(h), cols])).astype(jnp.bfloat16)
        back = copy(
            f"back_{name}", fin.at[half(h), cols], out_ref.at[half(h), cols], turn_peer
        )
        backs.append((h, back))

        @pl.when(jnp.logical_not(diagonal))
        def _():
            back.start()

    tiles = both // TILE
    cut = split_in // TILE

    def gate_up(e, then=None):
        ready(e)
        into_gate_up(e, 0, cut)
        reduce_1x(e)
        into_gate_up(e, cut, tiles)
        reduce_1y(e)
        if then is not None:
            forward(then)

    every = pl.ds(0, width)
    first(0)
    along_z(0)
    first(1)
    second(0)
    forward(0)
    w_copies[0].wait()
    w_copies[1].wait()
    ready(0)
    into_gate_up(0, 0, cut)
    reduce_1x(0)
    into_gate_up(0, cut, tiles)
    reduce_1y(0)
    second(1)
    forward(1)
    along_z(2)
    gate_up(1)
    reduce_2(0)
    forward(3)
    gate_up(3)
    reduce_2(1)
    reduce_2b(0)
    forward(2)
    gate_up(2)
    reduce_2(3)
    reduce_2b(1)
    reduce_3(0)
    reduce_2(2)
    reduce_2b(3)
    reduce_3(1)
    gather_2(0)
    reduce_2b(2)
    reduce_3(3)
    gather_2(1)
    gather_2b(0)
    reduce_3(2)
    gather_2(3)
    gather_2b(1)
    gather_2(2)
    gather_2b(3)
    w_copies[2].wait()
    down(0)
    down(1)
    gather_2b(2)
    out_2(0, 0, every)
    down(3)
    out_2(1, 1, every)

    piece = width // PIECES
    blocks = [pl.ds(i * piece, piece) for i in range(PIECES)]
    down_ready(2)
    for i, cols in enumerate(blocks):
        down_tiles(2, i * piece // TILE, (i + 1) * piece // TILE)
        send(f"oc_2{i}", obuf.at[2, 1 - k, :, :, cols], rcore.at[2, :, :, cols], core_peer)
        if i == 0:
            out_2(3, 3, every)
    for i, cols in enumerate(blocks):
        out_2(2, f"2{i}", cols)
        if i == 0:
            out_3(1, 1, every)
    out_3(3, 3, every)
    out_3(0, 0, every)
    for i, cols in enumerate(blocks):
        out_3(2, f"2{i}", cols)

    @pl.when(diagonal)
    def _():
        out_ref[...] = fin[...]

    for _, back in backs:

        @pl.when(jnp.logical_not(diagonal))
        def _():
            back.wait()

    for cp in sent:
        cp.wait_send()

    @pl.when(jnp.logical_not(diagonal))
    def _():
        turns[1].wait_send()

    for j in range(8):

        @pl.when(jnp.logical_not(jnp.logical_and(diagonal, j == r)))
        def _():
            sq_out[j].wait_send()


def feed_forward(index, residual, gain, gate_weight, up_weight, down_weight):
    rows, width = residual.shape
    hid = gate_weight.shape[1]
    both = 2 * hid
    split_in = both // TILE * 7 // 13 * TILE
    split_hid = hid // 128 * 6 // 13 * 128
    n_copies = 160
    cfg = dict(
        rows=rows,
        width=width,
        hid=hid,
        split_in=split_in,
        split_hid=split_hid,
        model=gain.shape[1],
        sq0=n_copies,
    )
    bf16 = jnp.bfloat16
    rest = both - split_in
    vmem = pl.BlockSpec(memory_space=pltpu.VMEM)
    hbm = pl.BlockSpec(memory_space=pl.ANY)
    scratch = [
        pltpu.VMEM((width, both), bf16),
        pltpu.VMEM((hid, width), bf16),
        pltpu.VMEM((1, width), jnp.float32),
        pltpu.VMEM((1, width), jnp.float32),
        pltpu.VMEM((8, 128), jnp.float32),
        pltpu.VMEM((rows, width), bf16),
        pltpu.VMEM((8, 8, 128), jnp.float32),
        pltpu.VMEM((4, 2, NZ, STRIPE, width), bf16),
        pltpu.VMEM((NZ, 2, NX, STRIPE, both), bf16),
        pltpu.VMEM((NZ, NX - 1, 2, STRIPE, split_in), bf16),
        pltpu.VMEM((NZ, 2, STRIPE, split_in), bf16),
        pltpu.VMEM((NZ, STRIPE, split_in), bf16),
        pltpu.VMEM((NZ, NX, STRIPE, rest), bf16),
        pltpu.VMEM((NZ, NX, STRIPE, rest), bf16),
        pltpu.VMEM((NZ, NX - 1, STRIPE, rest), bf16),
        pltpu.VMEM((NZ, 2, STRIPE, split_in), bf16),
        pltpu.VMEM((NZ, STRIPE, rest), bf16),
        pltpu.VMEM((NZ, 2, NX, STRIPE, hid), bf16),
        pltpu.VMEM((4, 2, NZ, STRIPE, width), bf16),
        pltpu.VMEM((4, NZ, STRIPE, width), bf16),
        pltpu.VMEM((4, NZ, STRIPE, width), bf16),
        pltpu.VMEM((4, NZ - 1, STRIPE, width), bf16),
        pltpu.VMEM((rows, width), bf16),
        pltpu.VMEM((rows, width), bf16),
        pltpu.VMEM((rows, width), bf16),
        pltpu.SemaphoreType.DMA((4,)),
        pltpu.SemaphoreType.DMA((n_copies + 8,)),
        pltpu.SemaphoreType.DMA((n_copies + 8,)),
        pltpu.SemaphoreType.DMA((2,)),
    ]
    return pl.pallas_call(
        functools.partial(ffn_kernel, cfg),
        out_shape=jax.ShapeDtypeStruct((rows, width), bf16),
        in_specs=[pl.BlockSpec(memory_space=pltpu.SMEM), vmem, hbm, hbm, hbm, hbm],
        out_specs=vmem,
        scratch_shapes=scratch,
        compiler_params=pltpu.CompilerParams(
            collective_id=0, has_side_effects=True, vmem_limit_bytes=60 * 2**20
        ),
    )(index, residual, gain, gate_weight, up_weight, down_weight)


def on_device(
    query_rows,
    key_cache,
    value_cache,
    cache_lengths,
    residual_in,
    norm_gain,
    outlier_index,
    gate_weight,
    up_weight,
    down_weight,
):
    rows_dev, width_dev = query_rows.shape
    cache_len = key_cache.shape[1]
    kv_local = key_cache.shape[2] // HD
    group_size = width_dev // HD // kv_local
    query_part = query_rows.reshape(rows_dev, kv_local, group_size, HD)
    key_part = key_cache.reshape(rows_dev, cache_len, kv_local, HD)
    value_part = value_cache.reshape(rows_dev, cache_len, kv_local, HD)
    scores = jnp.einsum(
        "igqd,itgd->igqt", query_part, key_part, preferred_element_type=jnp.float32
    ) * HD ** (-0.5)
    valid_mask = jnp.arange(cache_len, dtype=jnp.int32)[None, :] < cache_lengths[:, None]
    scores = jnp.where(valid_mask[:, None, None, :], scores, -1e30)
    top_score = jnp.max(scores, axis=-1, keepdims=True)
    expon = jnp.exp(scores - top_score)
    attn_probs = (expon / jnp.sum(expon, axis=-1, keepdims=True)).astype(jnp.bfloat16)
    attention = jnp.einsum(
        "igqt,itgd->igqd", attn_probs, value_part, preferred_element_type=jnp.float32
    ).reshape(rows_dev, width_dev)
    residual = (residual_in.astype(jnp.float32) + attention).astype(jnp.bfloat16)
    ffn = feed_forward(
        outlier_index, residual, norm_gain[None, :], gate_weight, up_weight, down_weight
    )
    return (residual.astype(jnp.float32) + ffn.astype(jnp.float32)).astype(jnp.bfloat16)


def solution(mesh):
    in_specs = (
        P(("side", "row"), "col"),
        P(("side", "row"), None, "col"),
        P(("side", "row"), None, "col"),
        P(("side", "row")),
        P(("side", "row"), "col"),
        P(),
        P(),
        P("row", ("side", "col")),
        P("row", ("side", "col")),
        P(("side", "col"), "row"),
    )
    out_specs = P(("side", "row"), "col")
    return jax.shard_map(
        on_device, mesh=mesh, in_specs=in_specs, out_specs=out_specs, check_vma=False
    )
```

```python
import functools

import jax
import jax.numpy as jnp
from jax import lax
from jax.experimental import pallas as pl
from jax.experimental.pallas import tpu as pltpu
from jax.sharding import PartitionSpec as P

HD = 128
MESH = pl.DeviceIdType.MESH
STRIPE = 16
TILE = 256
NX = 4
NZ = 4
ORDER = (0, 1, 3, 2)
RING = (0, 1, 3, 2)
PIECES = 2


def ffn_kernel(
    cfg,
    index_ref,
    res_ref,
    gain_hbm,
    gate_hbm,
    up_hbm,
    down_hbm,
    out_ref,
    w_in,
    w_out,
    gain_ref,
    mask_ref,
    sq_ref,
    turned,
    sq_buf,
    xbuf,
    gbuf,
    rx1,
    sx,
    rx2,
    ry1,
    sy,
    ry2,
    fx,
    fy,
    hbuf,
    obuf,
    rcore,
    osum,
    rz,
    fpeer,
    rside,
    fin,
    w_sem,
    send_sem,
    recv_sem,
    loc_sem,
):
    rows, width, hid = cfg["rows"], cfg["width"], cfg["hid"]
    split_in, split_hid = cfg["split_in"], cfg["split_hid"]
    both = 2 * hid
    s, r, c = lax.axis_index("side"), lax.axis_index("row"), lax.axis_index("col")
    x, p = r // 2, lax.rem(r, 2)
    z, k = c // 2, lax.rem(c, 2)
    diagonal = r == c

    def x_peer(d):
        return (s, lax.rem(x + d, NX) * 2 + p, c)

    def z_peer(d):
        return (s, r, lax.rem(z + d, NZ) * 2 + k)

    y_peer = (s, x * 2 + 1 - p, c)
    side_peer = (1 - s, r, c)
    core_peer = (s, r, z * 2 + 1 - k)
    turn_peer = (s, c, r)

    ids = {}

    def copy(name, src, dst, device):
        i = ids.setdefault(name, len(ids))
        return pltpu.make_async_remote_copy(
            src_ref=src,
            dst_ref=dst,
            send_sem=send_sem.at[i],
            recv_sem=recv_sem.at[i],
            device_id=device,
            device_id_type=MESH,
        )

    sent = []

    def send(name, src, dst, device):
        cp = copy(name, src, dst, device)
        cp.start()
        sent.append(cp)

    def arrive(name, dst):
        copy(name, dst, dst, core_peer).wait_recv()

    w_copies = [
        pltpu.make_async_copy(gate_hbm, w_in.at[:, pl.ds(0, hid)], w_sem.at[0]),
        pltpu.make_async_copy(up_hbm, w_in.at[:, pl.ds(hid, hid)], w_sem.at[1]),
        pltpu.make_async_copy(down_hbm, w_out, w_sem.at[2]),
    ]
    gain_copy = pltpu.make_async_copy(
        gain_hbm.at[:, pl.ds(pl.multiple_of(r * width, width), width)], gain_ref, w_sem.at[3]
    )
    gain_copy.start()
    for cp in w_copies:
        cp.start()

    barrier = pltpu.get_barrier_semaphore()
    greet = [x_peer(d) for d in range(1, NX)] + [z_peer(d) for d in range(1, NZ)]
    greet += [y_peer, side_peer, core_peer]
    for device in greet:
        pl.semaphore_signal(barrier, inc=1, device_id=device, device_id_type=MESH)
    for j in range(8):

        @pl.when(jnp.logical_not(jnp.logical_and(diagonal, j == r)))
        def _():
            pl.semaphore_signal(barrier, inc=1, device_id=(s, c, j), device_id_type=MESH)

    eye = lax.broadcasted_iota(jnp.int32, (rows, 128), 0) == lax.broadcasted_iota(
        jnp.int32, (rows, 128), 1
    )
    sq_part = jnp.sum(jnp.square(res_ref[...].astype(jnp.float32)), axis=1, keepdims=True)
    sq_ref[...] = jnp.broadcast_to(
        jnp.sum(jnp.where(eye, sq_part, 0.0), axis=0, keepdims=True), (8, 128)
    )
    pl.semaphore_wait(barrier, len(greet) + 8 - diagonal.astype(jnp.int32))

    def half(h):
        return pl.ds(h * STRIPE, STRIPE)

    turns = [
        copy(f"turn_{h}", res_ref.at[half(h)], turned.at[half(h)], turn_peer) for h in (0, 1)
    ]
    turn_here = pltpu.make_async_copy(res_ref, turned, loc_sem.at[0])
    sq_here = pltpu.make_async_copy(sq_ref, sq_buf.at[c], loc_sem.at[1])

    @pl.when(jnp.logical_not(diagonal))
    def _():
        turns[0].start()

    sq_out = []
    for j in range(8):
        cp = pltpu.make_async_remote_copy(
            src_ref=sq_ref,
            dst_ref=sq_buf.at[c],
            send_sem=send_sem.at[cfg["sq0"] + j],
            recv_sem=recv_sem.at[cfg["sq0"] + c],
            device_id=(s, j, r),
            device_id_type=MESH,
        )
        sq_out.append(cp)

        @pl.when(jnp.logical_not(jnp.logical_and(diagonal, j == r)))
        def _():
            cp.start()

    @pl.when(diagonal)
    def _():
        turn_here.start()
        sq_here.start()
        turn_here.wait()
        sq_here.wait()

    channel = lax.broadcasted_iota(jnp.int32, (1, width), 1) + r * width

    def match(j, found):
        return jnp.where(channel == index_ref[j], 1.0, found)

    mask_ref[...] = lax.fori_loop(
        0, index_ref.shape[0], match, jnp.zeros((1, width), jnp.float32), unroll=8
    )
    gain_copy.wait()

    @pl.when(jnp.logical_not(diagonal))
    def _():
        turns[0].wait_send()
        turns[1].start()

    for j in range(8):

        @pl.when(jnp.logical_not(jnp.logical_and(diagonal, j == c)))
        def _():
            pltpu.make_async_remote_copy(
                src_ref=sq_ref,
                dst_ref=sq_buf.at[j],
                send_sem=send_sem.at[cfg["sq0"] + j],
                recv_sem=recv_sem.at[cfg["sq0"] + j],
                device_id=core_peer,
                device_id_type=MESH,
            ).wait_recv()

    sq_row = jnp.sum(sq_buf[...], axis=0)[0:1, :]
    sq_col = jnp.sum(
        jnp.where(eye, jnp.broadcast_to(sq_row, (rows, 128)), 0.0), axis=1, keepdims=True
    )
    inv = 1.0 / jnp.sqrt(sq_col / cfg["model"] + 1e-5)

    def first(h):
        @pl.when(jnp.logical_not(diagonal))
        def _():
            turns[h].wait_recv()

        normed = turned[half(h)].astype(jnp.float32) * inv[h * STRIPE : (h + 1) * STRIPE]
        normed = normed * gain_ref[...]
        kept = jnp.where(mask_ref[...] > 0.5, normed, jnp.clip(normed, -3.0, 3.0))
        xbuf[2 * h, k, z] = kept.astype(jnp.bfloat16)
        send(f"g_s{h}", xbuf.at[2 * h, k, z], xbuf.at[2 * h + 1, k, z], side_peer)

    def along_z(e):
        for d in (2, 1, 3):
            send(f"g_z{e}_{d}", xbuf.at[e, k, z], xbuf.at[e, k, z], z_peer(d))

    def second(h):
        arrive(f"g_s{h}", xbuf.at[2 * h + 1, k, z])
        along_z(2 * h + 1)

    def forward(e):
        for d in (1, 3, 2):
            arrive(f"g_z{e}_{d}", xbuf.at[e, k, lax.rem(z + NZ - d, NZ)])
        send(f"g_c{e}", xbuf.at[e, k], xbuf.at[e, k], core_peer)

    def ready(e):
        arrive(f"g_c{e}", xbuf.at[e, 1 - k])

    def into_gate_up(e, lo, hi):
        for t in range(lo, hi):
            cols = pl.ds(t * TILE, TILE)
            part = jnp.dot(
                xbuf[e].reshape(4 * rows, width),
                w_in[:, cols],
                preferred_element_type=jnp.float32,
            )
            gbuf[e, :, :, :, cols] = part.astype(jnp.bfloat16).reshape(2, NX, STRIPE, TILE)

    left, right = pl.ds(0, split_in), pl.ds(split_in, both - split_in)

    def f32(value):
        return value.astype(jnp.float32)

    def halves(lo, size):
        mid = size // 256 * 128
        return pl.ds(lo, mid), pl.ds(lo + mid, size - mid)

    up, far, back_x = (lax.rem(x + d, NX) for d in (1, 2, 3))

    def ring_1(tag, src, land, a, b):
        send(tag + "fa", src(far, a), land(2, a), x_peer(1))
        send(tag + "fb", src(far, b), land(2, b), x_peer(3))
        send(tag + "ub", src(up, b), land(0, b), x_peer(1))
        send(tag + "da", src(back_x, a), land(1, a), x_peer(3))

    def ring_2(tag, src, land, stage, a, b):
        arrive(tag + "fa", land(2, a))
        stage(a)[...] = (f32(land(2, a)[...]) + f32(src(up, a)[...])).astype(jnp.bfloat16)
        send(tag + "ua", stage(a), land(0, a), x_peer(1))
        arrive(tag + "fb", land(2, b))
        stage(b)[...] = (f32(land(2, b)[...]) + f32(src(back_x, b)[...])).astype(jnp.bfloat16)
        send(tag + "db", stage(b), land(1, b), x_peer(3))

    def ring_3(tag, land, a, b):
        arrive(tag + "ub", land(0, b))
        arrive(tag + "da", land(1, a))
        arrive(tag + "ua", land(0, a))
        arrive(tag + "db", land(1, b))

    left_a, left_b = halves(0, split_in)
    rest_a, rest_b = halves(0, both - split_in)

    def x_first(e):
        return (
            f"rx1_{e}",
            lambda i, cols: gbuf.at[e, :, i, :, cols],
            lambda slot, cols: rx1.at[e, slot, :, :, cols],
            lambda cols: fx.at[e, :, :, cols],
        )

    def x_second(e):
        return (
            f"ry2_{e}",
            lambda i, cols: sy.at[e, i, :, cols],
            lambda slot, cols: ry2.at[e, slot, :, cols],
            lambda cols: fy.at[e, :, cols],
        )

    def reduce_1x(e):
        if e in RING:
            tag, src, land, _ = x_first(e)
            ring_1(tag, src, land, left_a, left_b)
            return
        for d in (2, 1, 3):
            send(
                f"rx1_{e}_{d}",
                gbuf.at[e, :, lax.rem(x + d, NX), :, left],
                rx1.at[e, d - 1],
                x_peer(d),
            )

    def reduce_1y(e):
        send(f"ry1_{e}", gbuf.at[e, 1 - p, :, :, right], ry1.at[e], y_peer)

    def x_total(e):
        slots = (0, 1) if e in RING else (0, 1, 2)

        def total(q):
            part = f32(gbuf[e, q, x, :, left])
            for slot in slots:
                part = part + f32(rx1[e, slot, q])
            return part.astype(jnp.bfloat16)

        sx[e, 1] = total(1 - p)
        send(f"rx2_{e}", sx.at[e, 1], rx2.at[e], y_peer)
        sx[e, 0] = total(p)

    def reduce_2(e):
        if e in RING:
            tag, src, land, stage = x_first(e)
            ring_2(tag, src, land, stage, left_a, left_b)
        arrive(f"ry1_{e}", ry1.at[e])
        sy[e] = (f32(gbuf[e, p, :, :, right]) + f32(ry1[e])).astype(jnp.bfloat16)
        if e in RING:
            tag, src, land, _ = x_second(e)
            ring_1(tag, src, land, rest_a, rest_b)
            return
        for d in (2, 1, 3):
            send(f"ry2_{e}_{d}", sy.at[e, lax.rem(x + d, NX)], ry2.at[e, d - 1], x_peer(d))
        for d in (1, 3, 2):
            arrive(f"rx1_{e}_{d}", rx1.at[e, d - 1])
        x_total(e)

    def reduce_2b(e):
        if e not in RING:
            return
        tag, _, land, _ = x_first(e)
        ring_3(tag, land, left_a, left_b)
        x_total(e)
        tag, src, land, stage = x_second(e)
        ring_2(tag, src, land, stage, rest_a, rest_b)

    act_a, act_b = pl.ds(0, split_hid), pl.ds(split_hid, hid - split_hid)
    act_aa, act_ab = halves(0, split_hid)
    act_ba, act_bb = halves(split_hid, hid - split_hid)

    def reduce_3(e):
        arrive(f"rx2_{e}", rx2.at[e])
        lower = f32(sx[e, 0]) + f32(rx2[e])
        upper = f32(sy[e, x])
        if e in RING:
            tag, _, land, _ = x_second(e)
            ring_3(tag, land, rest_a, rest_b)
        for d in (1, 2) if e in RING else (1, 2, 3):
            if e not in RING:
                arrive(f"ry2_{e}_{d}", ry2.at[e, d - 1])
            upper = upper + f32(ry2[e, d - 1])
        full = jnp.concatenate([lower, upper], axis=1)
        gate, up_sum = full[:, :hid], full[:, hid:]
        hbuf[e, p, x] = (gate / (1.0 + jnp.exp(-gate)) * up_sum).astype(jnp.bfloat16)
        for d in (1, 3) if e in RING else (2, 1, 3):
            send(f"hx1_{e}_{d}", hbuf.at[e, p, x, :, act_a], hbuf.at[e, p, x, :, act_a], x_peer(d))
        send(f"hy1_{e}", hbuf.at[e, p, x, :, act_b], hbuf.at[e, p, x, :, act_b], y_peer)

    def row_a(e, i, cols):
        return hbuf.at[e, p, i, :, cols]

    def row_b(e, i, cols):
        return hbuf.at[e, :, i, :, cols]

    def pass_on(e, tag, row, whole, a, b):
        arrive(f"{tag}_{e}_1", row(e, back_x, whole))
        send(f"{tag}_{e}_a", row(e, back_x, a), row(e, back_x, a), x_peer(1))
        arrive(f"{tag}_{e}_3", row(e, up, whole))
        send(f"{tag}_{e}_b", row(e, up, b), row(e, up, b), x_peer(3))

    def passed_on(e, tag, row, a, b):
        arrive(f"{tag}_{e}_a", row(e, far, a))
        arrive(f"{tag}_{e}_b", row(e, far, b))

    def gather_2(e):
        if e in RING:
            pass_on(e, "hx1", row_a, act_a, act_aa, act_ab)
        arrive(f"hy1_{e}", hbuf.at[e, 1 - p, x, :, act_b])
        for d in (1, 3) if e in RING else (2, 1, 3):
            send(f"hx2_{e}_{d}", row_b(e, x, act_b), row_b(e, x, act_b), x_peer(d))
        if e in RING:
            return
        for d in (1, 3, 2):
            arrive(f"hx1_{e}_{d}", row_a(e, lax.rem(x + NX - d, NX), act_a))
        send(f"hy2_{e}", hbuf.at[e, p, :, :, act_a], hbuf.at[e, p, :, :, act_a], y_peer)

    def gather_2b(e):
        if e not in RING:
            return
        passed_on(e, "hx1", row_a, act_aa, act_ab)
        send(f"hy2_{e}", hbuf.at[e, p, :, :, act_a], hbuf.at[e, p, :, :, act_a], y_peer)
        pass_on(e, "hx2", row_b, act_b, act_ba, act_bb)

    def down_ready(e):
        if e in RING:
            passed_on(e, "hx2", row_b, act_ba, act_bb)
        else:
            for d in (1, 3, 2):
                arrive(f"hx2_{e}_{d}", row_b(e, lax.rem(x + NX - d, NX), act_b))
        arrive(f"hy2_{e}", hbuf.at[e, 1 - p, :, :, act_a])

    def down_tiles(e, lo, hi):
        for t in range(lo, hi):
            cols = pl.ds(t * TILE, TILE)
            part = jnp.dot(
                hbuf[e].reshape(4 * rows, hid),
                w_out[:, cols],
                preferred_element_type=jnp.float32,
            )
            obuf[e, :, :, :, cols] = part.astype(jnp.bfloat16).reshape(2, NZ, STRIPE, TILE)

    def down(e):
        down_ready(e)
        down_tiles(e, 0, width // TILE)
        send(f"oc_{e}", obuf.at[e, 1 - k], rcore.at[e], core_peer)

    def out_2(e, name, cols):
        arrive(f"oc_{name}", rcore.at[e, :, :, cols])
        osum[e, :, :, cols] = (f32(obuf[e, k, :, :, cols]) + f32(rcore[e, :, :, cols])).astype(
            jnp.bfloat16
        )
        for d in (2, 1, 3):
            send(
                f"oz_{name}_{d}",
                osum.at[e, lax.rem(z + d, NZ), :, cols],
                rz.at[e, d - 1, :, cols],
                z_peer(d),
            )

    def z_sum(e, name, cols):
        part = f32(osum[e, z, :, cols])
        for d in (1, 3, 2):
            arrive(f"oz_{name}_{d}", rz.at[e, d - 1, :, cols])
            part = part + f32(rz[e, d - 1, :, cols])
        return part

    backs = []

    def out_3(e, name, cols):
        h, part = e // 2, z_sum(e, name, cols)
        if e % 2:
            fpeer[half(h), cols] = part.astype(jnp.bfloat16)
            send(f"os_{h}", fpeer.at[half(h), cols], rside.at[half(h), cols], side_peer)
            return
        if all(back_h != h for back_h, _ in backs):
            arrive(f"os_{h}", rside.at[half(h)])
        fin[half(h), cols] = (part + f32(rside[half(h), cols])).astype(jnp.bfloat16)
        back = copy(
            f"back_{name}", fin.at[half(h), cols], out_ref.at[half(h), cols], turn_peer
        )
        backs.append((h, back))

        @pl.when(jnp.logical_not(diagonal))
        def _():
            back.start()

    tiles = both // TILE
    cut = split_in // TILE

    def gate_up(e, then=None):
        ready(e)
        into_gate_up(e, 0, cut)
        reduce_1x(e)
        into_gate_up(e, cut, tiles)
        reduce_1y(e)
        if then is not None:
            forward(then)

    every = pl.ds(0, width)
    first(0)
    along_z(0)
    first(1)
    second(0)
    forward(0)
    w_copies[0].wait()
    w_copies[1].wait()
    ready(0)
    into_gate_up(0, 0, cut)
    reduce_1x(0)
    into_gate_up(0, cut, tiles)
    reduce_1y(0)
    second(1)
    forward(1)
    along_z(2)
    gate_up(1)
    reduce_2(0)
    forward(3)
    gate_up(3)
    reduce_2(1)
    reduce_2b(0)
    forward(2)
    gate_up(2)
    reduce_2(3)
    reduce_2b(1)
    reduce_3(0)
    reduce_2(2)
    reduce_2b(3)
    reduce_3(1)
    gather_2(0)
    reduce_2b(2)
    reduce_3(3)
    gather_2(1)
    gather_2b(0)
    reduce_3(2)
    gather_2(3)
    gather_2b(1)
    gather_2(2)
    gather_2b(3)
    w_copies[2].wait()
    down(0)
    down(1)
    gather_2b(2)
    out_2(0, 0, every)
    down(3)
    out_2(1, 1, every)

    piece = width // PIECES
    blocks = [pl.ds(i * piece, piece) for i in range(PIECES)]
    down_ready(2)
    for i, cols in enumerate(blocks):
        down_tiles(2, i * piece // TILE, (i + 1) * piece // TILE)
        send(f"oc_2{i}", obuf.at[2, 1 - k, :, :, cols], rcore.at[2, :, :, cols], core_peer)
        if i == 0:
            out_2(3, 3, every)
    for i, cols in enumerate(blocks):
        out_2(2, f"2{i}", cols)
        if i == 0:
            out_3(1, 1, every)
    out_3(3, 3, every)
    out_3(0, 0, every)
    for i, cols in enumerate(blocks):
        out_3(2, f"2{i}", cols)

    @pl.when(diagonal)
    def _():
        out_ref[...] = fin[...]

    for _, back in backs:

        @pl.when(jnp.logical_not(diagonal))
        def _():
            back.wait()

    for cp in sent:
        cp.wait_send()

    @pl.when(jnp.logical_not(diagonal))
    def _():
        turns[1].wait_send()

    for j in range(8):

        @pl.when(jnp.logical_not(jnp.logical_and(diagonal, j == r)))
        def _():
            sq_out[j].wait_send()


def feed_forward(index, residual, gain, gate_weight, up_weight, down_weight):
    rows, width = residual.shape
    hid = gate_weight.shape[1]
    both = 2 * hid
    split_in = both // TILE * 8 // 13 * TILE
    split_hid = hid // 128 * 5 // 13 * 128
    n_copies = 160
    cfg = dict(
        rows=rows,
        width=width,
        hid=hid,
        split_in=split_in,
        split_hid=split_hid,
        model=gain.shape[1],
        sq0=n_copies,
    )
    bf16 = jnp.bfloat16
    rest = both - split_in
    vmem = pl.BlockSpec(memory_space=pltpu.VMEM)
    hbm = pl.BlockSpec(memory_space=pl.ANY)
    scratch = [
        pltpu.VMEM((width, both), bf16),
        pltpu.VMEM((hid, width), bf16),
        pltpu.VMEM((1, width), jnp.float32),
        pltpu.VMEM((1, width), jnp.float32),
        pltpu.VMEM((8, 128), jnp.float32),
        pltpu.VMEM((rows, width), bf16),
        pltpu.VMEM((8, 8, 128), jnp.float32),
        pltpu.VMEM((4, 2, NZ, STRIPE, width), bf16),
        pltpu.VMEM((NZ, 2, NX, STRIPE, both), bf16),
        pltpu.VMEM((NZ, NX - 1, 2, STRIPE, split_in), bf16),
        pltpu.VMEM((NZ, 2, STRIPE, split_in), bf16),
        pltpu.VMEM((NZ, STRIPE, split_in), bf16),
        pltpu.VMEM((NZ, NX, STRIPE, rest), bf16),
        pltpu.VMEM((NZ, NX, STRIPE, rest), bf16),
        pltpu.VMEM((NZ, NX - 1, STRIPE, rest), bf16),
        pltpu.VMEM((NZ, 2, STRIPE, split_in), bf16),
        pltpu.VMEM((NZ, STRIPE, rest), bf16),
        pltpu.VMEM((NZ, 2, NX, STRIPE, hid), bf16),
        pltpu.VMEM((4, 2, NZ, STRIPE, width), bf16),
        pltpu.VMEM((4, NZ, STRIPE, width), bf16),
        pltpu.VMEM((4, NZ, STRIPE, width), bf16),
        pltpu.VMEM((4, NZ - 1, STRIPE, width), bf16),
        pltpu.VMEM((rows, width), bf16),
        pltpu.VMEM((rows, width), bf16),
        pltpu.VMEM((rows, width), bf16),
        pltpu.SemaphoreType.DMA((4,)),
        pltpu.SemaphoreType.DMA((n_copies + 8,)),
        pltpu.SemaphoreType.DMA((n_copies + 8,)),
        pltpu.SemaphoreType.DMA((2,)),
    ]
    return pl.pallas_call(
        functools.partial(ffn_kernel, cfg),
        out_shape=jax.ShapeDtypeStruct((rows, width), bf16),
        in_specs=[pl.BlockSpec(memory_space=pltpu.SMEM), vmem, hbm, hbm, hbm, hbm],
        out_specs=vmem,
        scratch_shapes=scratch,
        compiler_params=pltpu.CompilerParams(
            collective_id=0, has_side_effects=True, vmem_limit_bytes=60 * 2**20
        ),
    )(index, residual, gain, gate_weight, up_weight, down_weight)


def on_device(
    query_rows,
    key_cache,
    value_cache,
    cache_lengths,
    residual_in,
    norm_gain,
    outlier_index,
    gate_weight,
    up_weight,
    down_weight,
):
    rows_dev, width_dev = query_rows.shape
    cache_len = key_cache.shape[1]
    kv_local = key_cache.shape[2] // HD
    group_size = width_dev // HD // kv_local
    query_part = query_rows.reshape(rows_dev, kv_local, group_size, HD)
    key_part = key_cache.reshape(rows_dev, cache_len, kv_local, HD)
    value_part = value_cache.reshape(rows_dev, cache_len, kv_local, HD)
    scores = jnp.einsum(
        "igqd,itgd->igqt", query_part, key_part, preferred_element_type=jnp.float32
    ) * HD ** (-0.5)
    valid_mask = jnp.arange(cache_len, dtype=jnp.int32)[None, :] < cache_lengths[:, None]
    scores = jnp.where(valid_mask[:, None, None, :], scores, -1e30)
    top_score = jnp.max(scores, axis=-1, keepdims=True)
    expon = jnp.exp(scores - top_score)
    attn_probs = (expon / jnp.sum(expon, axis=-1, keepdims=True)).astype(jnp.bfloat16)
    attention = jnp.einsum(
        "igqt,itgd->igqd", attn_probs, value_part, preferred_element_type=jnp.float32
    ).reshape(rows_dev, width_dev)
    residual = (residual_in.astype(jnp.float32) + attention).astype(jnp.bfloat16)
    ffn = feed_forward(
        outlier_index, residual, norm_gain[None, :], gate_weight, up_weight, down_weight
    )
    return (residual.astype(jnp.float32) + ffn.astype(jnp.float32)).astype(jnp.bfloat16)


def solution(mesh):
    in_specs = (
        P(("side", "row"), "col"),
        P(("side", "row"), None, "col"),
        P(("side", "row"), None, "col"),
        P(("side", "row")),
        P(("side", "row"), "col"),
        P(),
        P(),
        P("row", ("side", "col")),
        P("row", ("side", "col")),
        P(("side", "col"), "row"),
    )
    out_specs = P(("side", "row"), "col")
    return jax.shard_map(
        on_device, mesh=mesh, in_specs=in_specs, out_specs=out_specs, check_vma=False
    )
```
